32 devices in a mesh: dom: 8 (over y, x, core), blk: 4 (over z).
Axes of the slice: x: 2, y: 2, z: 4, core: 2. Of those that a mesh axis runs over, the one named last changes fastest.
Arguments:
- displacement: float32 [3, 64, 32, 128], P(None, 'dom', 'blk'), may hold values from -6 to 6
- velocity: float32 [3, 64, 32, 128], P(None, 'dom', 'blk'), may hold values from -6 to 6
- load: float32 [3, 64, 32, 128], P(None, 'dom', 'blk'), may hold values from -6 to 6
- density: float32 [64, 32, 128], P('dom', 'blk'), may hold values from 0.5 to 1.5
- block_class: int32 [8, 4, 16], P('dom', 'blk'), may hold values from 0 to 2
- host_element: int32 [4, 32768], P('blk', 'dom'), may hold values from 0 to 7038, as said below
- host_coords: float32 [3, 4, 32768], P(None, 'blk', 'dom'), may hold values from 0 to 1
- fibre_slot: int32 [128, 4, 128], P('dom', 'blk'), may hold values from 0 to 4095, as said below
- fibre_angles: float32 [2, 128, 4, 128], P(None, 'dom', 'blk'), may hold values from -3.140625 to 3.140625
- fibre_stiffness: float32 [128, 4], P('dom', 'blk'), may hold values from 0.5 to 4
Outputs:
- new_displacement: float32 [3, 64, 32, 128], P(None, 'dom', 'blk')
- new_velocity: float32 [3, 64, 32, 128], P(None, 'dom', 'blk')
The draws below stay inside these ranges and needn't reach their ends.
Inputs may be any that keep to these rules, and one draw needn't show every extreme that they name: `host_element`: each entry is (i * 8 + j) * 128 + k with i < 7, j < 7, k < 127, a voxel element of the device's own block; a device's entries are laid out as 512 slots for each owner index along dom, in order. `fibre_slot`: the entries of one device are distinct; value // 512 is the dom index of the host device in the same blk column and value % 512 the slot among that host's 512 slots for this owner; on every device all 512 slots of one host are used.
All inputs are finite; a program needn't handle non-finite values.
Results may differ from the reference program's by a relative error of at most 0.0003.
Values sent between devices are 32-bit elements; how exact they have to be, the bound alone decides.
A program may use at most 64 MiB of HBM per device.

```python
import math
import jax
import jax.numpy as jnp
import numpy as np
from jax import lax

CX = 8
CY = 8
CZ = 128
FIB_DEV = 16
FNODES = 128
SLOTS = 4096
CAP = 512
NX = 64
NY = 32
FIB_ROWS = 128
N_DOM = 8
N_BLK = 4


def draw_host_element(key, part):
    key_x, key_y, key_z = jax.random.split(jax.random.fold_in(key, 7), 3)
    shape = (N_BLK, N_DOM * SLOTS)
    along_x = jax.random.randint(key_x, shape, 0, CX - 1)
    along_y = jax.random.randint(key_y, shape, 0, CY - 1)
    along_z = jax.random.randint(key_z, shape, 0, CZ - 1)
    flat = (along_x * CY + along_y) * CZ + along_z
    highest = ((CX - 2) * CY + (CY - 2)) * CZ + (CZ - 2)
    blocks = flat.reshape(N_BLK, N_DOM, SLOTS)
    blocks = blocks.at[:, :, 0].set(highest).at[:, :, 1].set(0)
    return blocks.reshape(shape).astype(jnp.int32)


def draw_fibre_slot(key, part):
    count = FIB_DEV * FNODES

    def single(sub):
        key_order, key_host, key_mix = jax.random.split(sub, 3)
        order = jax.random.permutation(key_order, SLOTS).astype(jnp.int32)
        chosen = jax.random.randint(key_host, (), 0, N_DOM)
        owner_block = jnp.arange(SLOTS, dtype=jnp.int32) // CAP
        priority = order + jnp.where(owner_block == chosen, SLOTS, 0).astype(jnp.int32)
        picked = lax.top_k(priority, count)[1].astype(jnp.int32)
        mixing = jax.random.permutation(key_mix, count)
        return picked[mixing]
    subs = jax.random.split(jax.random.fold_in(key, 11), N_DOM * N_BLK)
    table = jax.vmap(single)(subs)
    table = table.reshape(N_DOM, N_BLK, FIB_DEV, FNODES).transpose(0, 2, 1, 3)
    return table.reshape(N_DOM * FIB_DEV, N_BLK, FNODES).astype(jnp.int32)


def plant(drawn, own_key, smallest, top_value):
    longest = drawn.shape.index(max(drawn.shape))
    spots = []
    for shift in (0, 1):
        where = [jax.random.randint(jax.random.fold_in(own_key, axis), (), 0, length) for axis, length in enumerate(drawn.shape)]
        where[longest] = (where[longest] + shift) % drawn.shape[longest]
        spots.append(tuple(where))
    return drawn.at[spots[0]].set(smallest).at[spots[1]].set(top_value)


def levels(stream_key, extent, pieces, low, high):
    loudness, own = 1.0, jax.random.fold_in(stream_key, 6)
    for axis_at, parts in pieces:
        heights = jnp.exp(jax.random.uniform(jax.random.fold_in(own, axis_at), (parts,), jnp.float32, low / len(pieces), high / len(pieces)))
        loudness = loudness * jnp.repeat(heights, extent[axis_at] // parts).reshape([-1 if axis == axis_at else 1 for axis in range(len(extent))])
    return loudness


def normal_values(own_key, shape, scale, limit, shards=(), held_as=jnp.bfloat16):
    values = jax.random.normal(own_key, shape, jnp.float32) * scale
    if len(shards) > 0:
        values = levels(own_key, shape, shards, -0.22, 0.18) * values
    return jnp.clip(values, min=-limit, max=limit).astype(held_as)


def setup_inputs(seed: int = 0) -> dict:
    splits = jax.random.split(jax.random.key(seed), 11)
    displacement = normal_values(splits[0], (3, NX, NY, CZ), 1.0, 6.0, ((1, 8), (2, 4)), jnp.float32)
    velocity = normal_values(splits[1], (3, NX, NY, CZ), 1.0, 6.0, ((1, 8), (2, 4)), jnp.float32)
    load = normal_values(splits[2], (3, NX, NY, CZ), 1.0, 6.0, ((1, 8), (2, 4)), jnp.float32)
    density = jnp.clip(jnp.exp(math.log(1.5) - 1.0986123 * jax.random.uniform(splits[3], (NX, NY, CZ), jnp.float32) ** levels(splits[3], (NX, NY, CZ), ((0, 8), (1, 4)), -0.2, 0.2)), 0.5, 1.5)
    block_class = plant(jax.random.randint(splits[4], (NX // 8, NY // 8, CZ // 8), 0, 3), jax.random.fold_in(splits[4], 1), 0, 2).astype(jnp.int32)
    host_element = draw_host_element(jax.random.fold_in(splits[10], 71), 0)
    host_coords = jnp.clip(1.0 * jax.random.uniform(splits[6], (3, N_BLK, N_DOM * SLOTS), jnp.float32) ** levels(splits[6], (3, N_BLK, N_DOM * SLOTS), ((1, 4), (2, 8)), -0.2, 0.2), 0.0, 1.0)
    fibre_slot = draw_fibre_slot(jax.random.fold_in(splits[10], 71), 0)
    fibre_angles = jnp.clip(jax.random.uniform(splits[8], (2, FIB_ROWS, N_BLK, FNODES), jnp.float32, -3.140625, 3.140625), -3.140625, 3.140625)
    fibre_stiffness = jnp.clip(jnp.exp(math.log(4.0) - 2.0794415 * jax.random.uniform(splits[9], (FIB_ROWS, N_BLK), jnp.float32) ** levels(splits[9], (FIB_ROWS, N_BLK), ((0, 8), (1, 4)), -0.2, 0.2)), 0.5, 4.0)
    return {"displacement": displacement, "velocity": velocity, "load": load, "density": density, "block_class": block_class, "host_element": host_element, "host_coords": host_coords, "fibre_slot": fibre_slot, "fibre_angles": fibre_angles, "fibre_stiffness": fibre_stiffness}


class_values = (1.0, 0.45, 0.12)
time_step = 0.25
damping = 0.5

def stiffness_table():
    poisson = 0.3
    lame = poisson / ((1 + poisson) * (1 - 2 * poisson))
    shear = 0.5 / (1 + poisson)
    elastic = np.zeros((6, 6))
    elastic[:3, :3] = lame
    for place in range(3):
        elastic[place, place] += 2 * shear
        elastic[place + 3, place + 3] = shear
    points = [0.5 - 0.5 / np.sqrt(3.0), 0.5 + 0.5 / np.sqrt(3.0)]
    table = np.zeros((24, 24))
    for gauss_r in points:
        for gauss_p in points:
            for gauss_q in points:
                strain = np.zeros((6, 24))
                for corner in range(8):
                    x_bit, y_bit, z_bit = (corner // 4, corner // 2 % 2, corner % 2)
                    along_r = gauss_r if x_bit else 1 - gauss_r
                    along_p = gauss_p if y_bit else 1 - gauss_p
                    along_q = gauss_q if z_bit else 1 - gauss_q
                    d_x = (2 * x_bit - 1) * along_p * along_q
                    d_y = along_r * (2 * y_bit - 1) * along_q
                    d_z = along_r * along_p * (2 * z_bit - 1)
                    column = 3 * corner
                    strain[0, column] = d_x
                    strain[1, column + 1] = d_y
                    strain[2, column + 2] = d_z
                    strain[3, column] = d_y
                    strain[3, column + 1] = d_x
                    strain[4, column + 1] = d_z
                    strain[4, column + 2] = d_y
                    strain[5, column] = d_z
                    strain[5, column + 2] = d_x
                table += 0.125 * strain.T @ elastic @ strain
    return table

def class_moduli(block_class):
    factor = jnp.zeros(block_class.shape, jnp.float32)
    for index, value in enumerate(class_values):
        factor = factor + jnp.where(block_class == index, jnp.float32(value), jnp.float32(0.0))
    bx, by, bz = block_class.shape
    wide = jnp.broadcast_to(factor[:, None, :, None, :, None], (bx, 8, by, 8, bz, 8))
    return wide.reshape(bx * 8, by * 8, bz * 8)

def lift_depth(local):
    return jnp.concatenate([local[..., 1:], jnp.zeros_like(local[..., :1])], axis=-1)

def element_forces(padded, moduli, density):
    width = padded.shape[1] - 2
    height = padded.shape[2] - 2
    depth = padded.shape[3]
    table = jnp.asarray(stiffness_table(), jnp.float32)
    element = jnp.zeros((24, width + 1, height + 1, depth), jnp.float32)
    for corner in range(8):
        x_bit, y_bit, z_bit = (corner // 4, corner // 2 % 2, corner % 2)
        local = padded[:, x_bit:x_bit + width + 1, y_bit:y_bit + height + 1, :]
        if z_bit:
            local = lift_depth(local)
        element = element + jnp.einsum('ij,jxyz->ixyz', table[:, 3 * corner:3 * corner + 3], local, precision=lax.Precision.HIGHEST)
    element = element * moduli[None, :width + 1, :height + 1, :]
    weight = density[:width + 1, :height + 1, :]
    force = jnp.zeros((3, width, height, depth), jnp.float32)
    mass = jnp.zeros((width, height, depth), jnp.float32)
    for corner in range(8):
        x_bit, y_bit, z_bit = (corner // 4, corner // 2 % 2, corner % 2)
        piece = element[3 * corner:3 * corner + 3, 1 - x_bit:1 - x_bit + width, 1 - y_bit:1 - y_bit + height, :]
        share = weight[1 - x_bit:1 - x_bit + width, 1 - y_bit:1 - y_bit + height, :]
        if z_bit:
            piece = jnp.pad(piece[..., :-1], ((0, 0), (0, 0), (0, 0), (1, 0)))
            share = jnp.pad(share[..., :-1], ((0, 0), (0, 0), (1, 0)))
        force = force + piece
        mass = mass + 0.125 * share
    return (force, mass)

def corner_table(element, coords, height, depth):
    rows = []
    weights = []
    for corner in range(8):
        x_bit, y_bit, z_bit = (corner // 4, corner // 2 % 2, corner % 2)
        rows.append(element + (x_bit * height * depth + y_bit * depth + z_bit))
        along_r = coords[0] if x_bit else 1.0 - coords[0]
        along_p = coords[1] if y_bit else 1.0 - coords[1]
        along_q = coords[2] if z_bit else 1.0 - coords[2]
        weights.append(along_r * along_p * along_q)
    return (jnp.stack(rows).astype(jnp.int32), jnp.stack(weights))

def interpolate(field, element, coords, height, depth):
    indices, weights = corner_table(element, coords, height, depth)
    gathered = field[:, indices]
    return lax.optimization_barrier(jnp.sum(gathered * weights[None], axis=1))

def spread(force, element, coords, count, height, depth):
    indices, weights = corner_table(element, coords, height, depth)
    terms = force[:, None, :] * weights[None]
    return jnp.zeros((3, count), jnp.float32).at[:, indices].add(terms)

def fibre_forces(places, slots, angles, stiffness):
    node = places[:, slots]
    direction = jnp.stack([jnp.cos(angles[0]) * jnp.cos(angles[1]), jnp.sin(angles[0]) * jnp.cos(angles[1]), jnp.sin(angles[1])])
    ahead = jnp.concatenate([node[..., 1:], node[..., -1:]], axis=-1)
    strain = lax.optimization_barrier(jnp.sum(direction * (ahead - node), axis=0))
    live = lax.broadcasted_iota(jnp.int32, strain.shape, 1) < strain.shape[1] - 1
    tension = jnp.where(live, stiffness * jnp.maximum(strain, 0.0), jnp.float32(0.0))
    pull = tension[None] * direction
    behind = jnp.concatenate([jnp.zeros_like(pull[..., :1]), pull[..., :-1]], axis=-1)
    return jnp.zeros(places.shape, jnp.float32).at[:, slots].set(pull - behind)

def reference(displacement, velocity, load, density, block_class, host_element, host_coords, fibre_slot, fibre_angles, fibre_stiffness):
    moduli = class_moduli(block_class) * density * density
    padded_field = jnp.pad(displacement, ((0, 0), (1, 1), (1, 1), (0, 0)))
    padded_moduli = jnp.pad(moduli, ((1, 1), (1, 1), (0, 0)))
    padded_density = jnp.pad(density, ((1, 1), (1, 1), (0, 0)))

    def slab(start):
        return element_forces(lax.dynamic_slice_in_dim(padded_field, start, CX + 2, 1), lax.dynamic_slice_in_dim(padded_moduli, start, CX + 2, 0), lax.dynamic_slice_in_dim(padded_density, start, CX + 2, 0))
    starts = jnp.arange(N_DOM, dtype=jnp.int32) * CX
    slab_force, slab_mass = lax.map(slab, starts)
    elastic = slab_force.transpose(1, 0, 2, 3, 4).reshape(3, NX, NY, CZ)
    mass = slab_mass.reshape(NX, NY, CZ)
    count = N_DOM * N_BLK
    blocks = displacement.reshape(3, N_DOM, CX, N_BLK, CY, CZ).transpose(1, 3, 0, 2, 4, 5).reshape(count, 3, CX * CY * CZ)
    elements = host_element.reshape(N_BLK, N_DOM, SLOTS).transpose(1, 0, 2).reshape(count, SLOTS)
    coords = host_coords.reshape(3, N_BLK, N_DOM, SLOTS).transpose(2, 1, 0, 3).reshape(count, 3, SLOTS)

    def host_places(item):
        return interpolate(item[0], item[1], item[2], CY, CZ)
    places = lax.map(host_places, (blocks, elements, coords))
    owned = places.reshape(N_DOM, N_BLK, 3, N_DOM, CAP).transpose(3, 1, 2, 0, 4).reshape(count, 3, SLOTS)
    slots = fibre_slot.reshape(N_DOM, FIB_DEV, N_BLK, FNODES).transpose(0, 2, 1, 3).reshape(count, FIB_DEV, FNODES)
    angles = fibre_angles.reshape(2, N_DOM, FIB_DEV, N_BLK, FNODES).transpose(1, 3, 0, 2, 4).reshape(count, 2, FIB_DEV, FNODES)
    stiffness = fibre_stiffness.reshape(N_DOM, FIB_DEV, N_BLK).transpose(0, 2, 1).reshape(count, FIB_DEV, 1)
    pulls = jax.vmap(fibre_forces)(owned, slots, angles, stiffness)
    hosted = pulls.reshape(N_DOM, N_BLK, 3, N_DOM, CAP).transpose(3, 1, 2, 0, 4).reshape(count, 3, SLOTS)

    def host_spread(item):
        return spread(item[0], item[1], item[2], CX * CY * CZ, CY, CZ)
    spreads = lax.map(host_spread, (hosted, elements, coords))
    fibre = spreads.reshape(N_DOM, N_BLK, 3, CX, CY, CZ).transpose(2, 0, 3, 1, 4, 5).reshape(3, NX, NY, CZ)
    acceleration = (load - elastic + fibre) / mass[None] - damping * velocity
    new_velocity = velocity + time_step * acceleration
    new_displacement = displacement + time_step * new_velocity
    return (new_displacement, new_velocity)
```

```python
import math

import jax
import jax.numpy as jnp
import numpy as np
from jax import lax
from jax.sharding import PartitionSpec as P

class_values = (1.0, 0.45, 0.12)
time_step = 0.25
damping = 0.5


def padded_2(block, sides, width):
    for axis, dim in sides:
        count = lax.axis_size(axis)
        forward = [(i, i + 1) for i in range(count - 1)]
        backward = [(target, source) for source, target in forward]
        low = lax.ppermute(
            lax.slice_in_dim(block, block.shape[dim] - width, None, axis=dim), axis, forward
        )
        high = lax.ppermute(lax.slice_in_dim(block, 0, width, axis=dim), axis, backward)
        block = jnp.concatenate([low, block, high], axis=dim)
    return block


def stiffness_table():
    poisson = 0.3
    lame = poisson / ((1 + poisson) * (1 - 2 * poisson))
    shear = 0.5 / (1 + poisson)
    elastic = np.zeros((6, 6))
    elastic[:3, :3] = lame
    for place in range(3):
        elastic[place, place] += 2 * shear
        elastic[place + 3, place + 3] = shear
    points = [0.5 - 0.5 / np.sqrt(3.0), 0.5 + 0.5 / np.sqrt(3.0)]
    table = np.zeros((24, 24))
    for gauss_r in points:
        for gauss_p in points:
            for gauss_q in points:
                strain = np.zeros((6, 24))
                for corner in range(8):
                    x_bit, y_bit, z_bit = (corner // 4, corner // 2 % 2, corner % 2)
                    along_r = gauss_r if x_bit else 1 - gauss_r
                    along_p = gauss_p if y_bit else 1 - gauss_p
                    along_q = gauss_q if z_bit else 1 - gauss_q
                    d_x = (2 * x_bit - 1) * along_p * along_q
                    d_y = along_r * (2 * y_bit - 1) * along_q
                    d_z = along_r * along_p * (2 * z_bit - 1)
                    column = 3 * corner
                    strain[0, column] = d_x
                    strain[1, column + 1] = d_y
                    strain[2, column + 2] = d_z
                    strain[3, column] = d_y
                    strain[3, column + 1] = d_x
                    strain[4, column + 1] = d_z
                    strain[4, column + 2] = d_y
                    strain[5, column] = d_z
                    strain[5, column + 2] = d_x
                table += 0.125 * strain.T @ elastic @ strain
    return table


def class_moduli(block_class):
    factor = jnp.zeros(block_class.shape, jnp.float32)
    for index, value in enumerate(class_values):
        factor = factor + jnp.where(block_class == index, jnp.float32(value), jnp.float32(0.0))
    bx, by, bz = block_class.shape
    wide = jnp.broadcast_to(factor[:, None, :, None, :, None], (bx, 8, by, 8, bz, 8))
    return wide.reshape(bx * 8, by * 8, bz * 8)


def lift_depth(local):
    return jnp.concatenate([local[..., 1:], jnp.zeros_like(local[..., :1])], axis=-1)


def element_forces(padded, moduli, density):
    width = padded.shape[1] - 2
    height = padded.shape[2] - 2
    depth = padded.shape[3]
    table = jnp.asarray(stiffness_table(), jnp.float32)
    element = jnp.zeros((24, width + 1, height + 1, depth), jnp.float32)
    for corner in range(8):
        x_bit, y_bit, z_bit = (corner // 4, corner // 2 % 2, corner % 2)
        local = padded[:, x_bit : x_bit + width + 1, y_bit : y_bit + height + 1, :]
        if z_bit:
            local = lift_depth(local)
        element = element + jnp.einsum(
            "ij,jxyz->ixyz",
            table[:, 3 * corner : 3 * corner + 3],
            local,
            precision=lax.Precision.HIGHEST,
        )
    element = element * moduli[None, : width + 1, : height + 1, :]
    weight = density[: width + 1, : height + 1, :]
    force = jnp.zeros((3, width, height, depth), jnp.float32)
    mass = jnp.zeros((width, height, depth), jnp.float32)
    for corner in range(8):
        x_bit, y_bit, z_bit = (corner // 4, corner // 2 % 2, corner % 2)
        piece = element[
            3 * corner : 3 * corner + 3,
            1 - x_bit : 1 - x_bit + width,
            1 - y_bit : 1 - y_bit + height,
            :,
        ]
        share = weight[1 - x_bit : 1 - x_bit + width, 1 - y_bit : 1 - y_bit + height, :]
        if z_bit:
            piece = jnp.pad(piece[..., :-1], ((0, 0), (0, 0), (0, 0), (1, 0)))
            share = jnp.pad(share[..., :-1], ((0, 0), (0, 0), (1, 0)))
        force = force + piece
        mass = mass + 0.125 * share
    return (force, mass)


def axis_weights(along, lowest, count):
    positions = lax.broadcasted_iota(jnp.int32, (count, along.shape[0]), 0)
    lower = jnp.where(positions == lowest[None], 1.0 - along[None], jnp.float32(0.0))
    upper = jnp.where(positions == lowest[None] + 1, along[None], jnp.float32(0.0))
    return lower + upper


def slot_weights(element, coords, width, height, depth):
    plane = height * depth
    along_x = element // plane
    along_y = element // depth % height
    along_z = element % depth
    weight_x = axis_weights(coords[0], along_x, width)
    weight_y = axis_weights(coords[1], along_y, height)
    weight_z = axis_weights(coords[2], along_z, depth)
    planar = (weight_x[:, None, :] * weight_y[None]).reshape(width * height, -1)
    return (planar, weight_z)


def interpolate(field, planar, weight_z):
    width, height, depth = (field.shape[1], field.shape[2], field.shape[3])
    partial_sums = jnp.dot(
        field.reshape(3 * width * height, depth), weight_z, precision=lax.Precision.HIGHEST
    )
    return jnp.sum(partial_sums.reshape(3, width * height, -1) * planar[None], axis=1)


def spread(force, planar, weight_z, width, height, depth):
    terms = (force[:, None, :] * planar[None]).reshape(3 * width * height, -1)
    summed = jnp.dot(terms, weight_z.T, precision=lax.Precision.HIGHEST)
    return summed.reshape(3, width, height, depth)


def split_onehots(wanted, total):
    lanes = math.gcd(total, 128)
    low = (
        lax.broadcasted_iota(jnp.int32, (lanes, wanted.shape[0]), 0) == (wanted % lanes)[None]
    ).astype(jnp.float32)
    high = lax.broadcasted_iota(jnp.int32, (total // lanes, wanted.shape[0]), 0) == (
        wanted // lanes
    )[None]
    return low, high


def pick_rows(places, wanted, span_rows):
    total = places.shape[1]
    low, high = split_onehots(wanted, total)
    rows, lanes = high.shape[0], low.shape[0]
    spread_rows = jnp.dot(places.reshape(3 * rows, lanes), low, precision=lax.Precision.HIGHEST)
    return jnp.sum(jnp.where(high[None], spread_rows.reshape(3, rows, -1), 0.0), axis=1)


def place_rows(values, wanted, total, span_rows):
    low, high = split_onehots(wanted, total)
    rows, lanes = high.shape[0], low.shape[0]
    terms = jnp.where(high[None], values[:, None, :], 0.0).reshape(3 * rows, -1)
    return jnp.dot(terms, low.T, precision=lax.Precision.HIGHEST).reshape(3, total)


def fibre_forces(places, slots, angles, stiffness):
    total = places.shape[1]
    fibres, nodes = slots.shape
    wanted = slots.reshape(-1)
    span_rows = math.gcd(fibres * nodes, 512)
    node = pick_rows(places, wanted, span_rows).reshape(3, fibres, nodes)
    direction = jnp.stack(
        [
            jnp.cos(angles[0]) * jnp.cos(angles[1]),
            jnp.sin(angles[0]) * jnp.cos(angles[1]),
            jnp.sin(angles[1]),
        ]
    )
    ahead = jnp.concatenate([node[..., 1:], node[..., -1:]], axis=-1)
    strain = jnp.sum(direction * (ahead - node), axis=0)
    live = lax.broadcasted_iota(jnp.int32, strain.shape, 1) < strain.shape[1] - 1
    tension = jnp.where(live, stiffness * jnp.maximum(strain, 0.0), jnp.float32(0.0))
    pull = tension[None] * direction
    behind = jnp.concatenate([jnp.zeros_like(pull[..., :1]), pull[..., :-1]], axis=-1)
    return place_rows((pull - behind).reshape(3, -1), wanted, total, span_rows)


def shards(
    displacement,
    velocity,
    load,
    density,
    block_class,
    host_element,
    host_coords,
    fibre_slot,
    fibre_angles,
    fibre_stiffness,
):
    width, height, depth = (displacement.shape[1], displacement.shape[2], displacement.shape[3])
    parts = lax.axis_size("dom")
    moduli = class_moduli(block_class) * density * density
    element = host_element[0]
    coords = host_coords[:, 0]
    planar, weight_z = slot_weights(element, coords, width, height, depth)
    places = interpolate(displacement, planar, weight_z)
    received = lax.all_to_all(
        places.reshape(3, parts, -1), "dom", split_axis=1, concat_axis=1, tiled=True
    )
    pulls = fibre_forces(
        received.reshape(3, -1), fibre_slot[:, 0], fibre_angles[:, :, 0], fibre_stiffness
    )
    returned = lax.all_to_all(
        pulls.reshape(3, parts, -1), "dom", split_axis=1, concat_axis=1, tiled=True
    )
    fibre = spread(returned.reshape(3, -1), planar, weight_z, width, height, depth)
    fields = jnp.concatenate([displacement, moduli[None], density[None]], axis=0)
    padded = padded_2(fields, (("dom", 1), ("blk", 2)), 1)
    elastic, mass = element_forces(padded[:3], padded[3], padded[4])
    acceleration = (load - elastic + fibre) / mass[None] - damping * velocity
    new_velocity = velocity + time_step * acceleration
    new_displacement = displacement + time_step * new_velocity
    return (new_displacement, new_velocity)


def solution(mesh):
    return jax.shard_map(
        shards,
        mesh=mesh,
        in_specs=(
            P(None, "dom", "blk", None),
            P(None, "dom", "blk", None),
            P(None, "dom", "blk", None),
            P("dom", "blk", None),
            P("dom", "blk", None),
            P("blk", "dom"),
            P(None, "blk", "dom"),
            P("dom", "blk", None),
            P(None, "dom", "blk", None),
            P("dom", "blk"),
        ),
        out_specs=(P(None, "dom", "blk", None), P(None, "dom", "blk", None)),
        check_vma=False,
    )
```

```python
import functools

import jax
import jax.numpy as jnp
import numpy as np
from jax import lax
from jax.experimental import pallas as pl
from jax.experimental.pallas import tpu as pltpu
from jax.sharding import PartitionSpec as P

class_values = (1.0, 0.45, 0.12)
time_step = 0.25
damping = 0.5
block_edge = 8
lanes = 128
MESH = pl.DeviceIdType.MESH


def stiffness_table():
    poisson = 0.3
    lame = poisson / ((1 + poisson) * (1 - 2 * poisson))
    shear = 0.5 / (1 + poisson)
    elastic = np.zeros((6, 6))
    elastic[:3, :3] = lame
    for place in range(3):
        elastic[place, place] += 2 * shear
        elastic[place + 3, place + 3] = shear
    points = [0.5 - 0.5 / np.sqrt(3.0), 0.5 + 0.5 / np.sqrt(3.0)]
    table = np.zeros((24, 24))
    for gauss_r in points:
        for gauss_p in points:
            for gauss_q in points:
                strain = np.zeros((6, 24))
                for corner in range(8):
                    x_bit, y_bit, z_bit = (corner // 4, corner // 2 % 2, corner % 2)
                    along_r = gauss_r if x_bit else 1 - gauss_r
                    along_p = gauss_p if y_bit else 1 - gauss_p
                    along_q = gauss_q if z_bit else 1 - gauss_q
                    d_x = (2 * x_bit - 1) * along_p * along_q
                    d_y = along_r * (2 * y_bit - 1) * along_q
                    d_z = along_r * along_p * (2 * z_bit - 1)
                    column = 3 * corner
                    strain[0, column] = d_x
                    strain[1, column + 1] = d_y
                    strain[2, column + 2] = d_z
                    strain[3, column] = d_y
                    strain[3, column + 1] = d_x
                    strain[4, column + 1] = d_z
                    strain[4, column + 2] = d_y
                    strain[5, column] = d_z
                    strain[5, column + 2] = d_x
                table += 0.125 * strain.T @ elastic @ strain
    return table


def mode_stiffness():
    single = np.linalg.inv(np.array([[1.0, 1.0], [-1.0, 1.0]]))
    back = np.kron(np.kron(np.kron(single, single), single), np.eye(3))
    table = back.T @ stiffness_table() @ back
    return np.where(np.abs(table) < 1e-12, 0.0, table)


def halves(value):
    high = value.astype(jnp.bfloat16)
    low = (value - high.astype(jnp.float32)).astype(jnp.bfloat16)
    return high, low


def quotient(value, divisor):
    if divisor & (divisor - 1) == 0:
        return lax.shift_right_logical(value, jnp.full_like(value, divisor.bit_length() - 1))
    return lax.div(value, jnp.full_like(value, divisor))


def dot(left, right):
    return jnp.dot(left, right, preferred_element_type=jnp.float32)


def dot_t(left, right):
    return lax.dot_general(
        left, right, (((1,), (1,)), ((), ())), preferred_element_type=jnp.float32
    )


def kernel(
    parts,
    columns,
    class_ref,
    displacement_ref,
    velocity_ref,
    load_ref,
    density_ref,
    element_ref,
    coords_ref,
    slot_ref,
    angle_ref,
    stiffness_ref,
    new_displacement_ref,
    new_velocity_ref,
    fields,
    y_send,
    y_recv,
    x_recv,
    weight_z,
    weight_x,
    weight_y,
    onehot,
    angles,
    picked,
    nodes,
    send_out,
    recv_out,
    send_back,
    recv_back,
    total,
    elastic,
    mass,
    y_sems,
    x_sems,
    out_send_sems,
    out_recv_sems,
    back_send_sems,
    back_recv_sems,
):
    _, width, height, depth = displacement_ref.shape
    rows = fields.shape[2]
    cap = recv_out.shape[2]
    slot_rows = cap // lanes
    all_rows = parts * slot_rows
    fibres = slot_ref.shape[0]
    me = lax.axis_index("dom")
    column = lax.axis_index("blk")

    barrier = pltpu.get_barrier_semaphore()

    def greet(step, carry):
        other = lax.rem(me + step, parts)
        pl.semaphore_signal(barrier, inc=1, device_id=(other, column), device_id_type=MESH)
        return carry

    lax.fori_loop(1, parts, greet, 0)

    @pl.when(column > 0)
    def _():
        pl.semaphore_signal(barrier, inc=1, device_id=(me, column - 1), device_id_type=MESH)

    @pl.when(column < columns - 1)
    def _():
        pl.semaphore_signal(barrier, inc=1, device_id=(me, column + 1), device_id_type=MESH)

    block_of = quotient(lax.broadcasted_iota(jnp.int32, (1, depth), 1), block_edge)
    for x in range(width):
        for y_block in range(height // block_edge):
            classes = jnp.zeros((1, depth), jnp.int32)
            for z_block in range(depth // block_edge):
                classes = jnp.where(
                    block_of == z_block, class_ref[x // block_edge, y_block, z_block], classes
                )
            factor = jnp.zeros((1, depth), jnp.float32)
            for index, value in enumerate(class_values):
                factor = jnp.where(classes == index, jnp.float32(value), factor)
            span = slice(y_block * block_edge, (y_block + 1) * block_edge)
            density = density_ref[x, span, :]
            fields[x + 1, 3, span, :] = factor * density * density
            fields[x + 1, 4, span, :] = density
    blank = jnp.zeros((rows - height, depth), jnp.float32)
    for x in range(width):
        for field in range(3):
            fields[x + 1, field, 0:height, :] = displacement_ref[field, x]
        for field in range(5):
            fields[x + 1, field, height:rows, :] = blank
    for x in range(width):
        for field in range(5):
            y_send[0, field, x : x + 1, :] = fields[x + 1, field, 0:1, :]
            y_send[1, field, x : x + 1, :] = fields[x + 1, field, height - 1 : height, :]

    def weigh(part, carry):
        span = pl.ds(pl.multiple_of(part * cap, lanes), cap)
        element = element_ref[:, span]
        along_x = quotient(element, height * depth)
        along_y = quotient(element - along_x * (height * depth), depth)
        along_z = element - along_x * (height * depth) - along_y * depth

        def weights(lowest, along, count):
            positions = lax.broadcasted_iota(jnp.int32, (count, cap), 0)
            upper = jnp.where(positions == lowest + 1, along, 0.0)
            return jnp.where(positions == lowest, 1.0 - along, upper)

        weight_x[:, span] = weights(along_x, coords_ref[0, :, span], width)
        weight_y[:, span] = weights(along_y, coords_ref[1, :, span], height)
        high, low = halves(weights(along_z, coords_ref[2, :, span], depth))
        weight_z[0:depth, span] = high
        weight_z[depth : 2 * depth, span] = low
        return carry

    lax.fori_loop(0, parts, weigh, 0)

    def barrier_count():
        return (
            parts
            - 1
            + jnp.where(column > 0, 1, 0)
            + jnp.where(column < columns - 1, 1, 0)
        )

    pl.semaphore_wait(barrier, barrier_count())

    def y_copy(side):
        return pltpu.make_async_remote_copy(
            src_ref=y_send.at[side],
            dst_ref=y_recv.at[1 - side],
            send_sem=y_sems.at[side],
            recv_sem=y_sems.at[3 - side],
            device_id=(me, column - 1 if side == 0 else column + 1),
            device_id_type=MESH,
        )

    def x_copy(side):
        return pltpu.make_async_remote_copy(
            src_ref=fields.at[1 if side == 0 else width],
            dst_ref=x_recv.at[1 - side],
            send_sem=x_sems.at[side],
            recv_sem=x_sems.at[3 - side],
            device_id=(me - 1 if side == 0 else me + 1, column),
            device_id_type=MESH,
        )

    y_there = (column > 0, column < columns - 1)
    x_there = (me > 0, me < parts - 1)
    for side in range(2):

        @pl.when(y_there[side])
        def _():
            y_copy(side).start()

    def slot_copy(source, target, send_sems, recv_sems, other, slot):
        return pltpu.make_async_remote_copy(
            src_ref=source.at[other],
            dst_ref=target.at[slot],
            send_sem=send_sems.at[other],
            recv_sem=recv_sems.at[slot],
            device_id=(other, column),
            device_id_type=MESH,
        )

    high, low = halves(displacement_ref[...].reshape(3 * width * height, depth))
    high = jnp.concatenate([high, high], axis=1)
    low = jnp.concatenate([low, low], axis=1)

    def planar_weights(span):
        planar = weight_x[:, span][:, None, :] * weight_y[:, span][None]
        return planar.reshape(width * height, cap)

    def interpolate(step, carry):
        other = lax.rem(me + step, parts)
        span = pl.ds(pl.multiple_of(other * cap, lanes), cap)
        weight = weight_z[:, span]
        sums = dot(high, weight) + dot(low, weight)
        planar = planar_weights(span)
        for field in range(3):
            piece = sums[field * width * height : (field + 1) * width * height]
            send_out[other, field : field + 1, :] = jnp.sum(piece * planar, axis=0, keepdims=True)

        @pl.when(other != me)
        def _():
            slot_copy(send_out, recv_out, out_send_sems, out_recv_sems, other, me).start()

        return carry

    lax.fori_loop(1, parts + 1, interpolate, 0)
    recv_out[me] = send_out[me]

    slots = jnp.concatenate([slot_ref[fibre] for fibre in range(fibres)], axis=1)
    slot_row = quotient(slots, lanes)
    slot_lane = slots - slot_row * lanes
    lane_count = lax.broadcasted_iota(jnp.int32, (lanes, slots.shape[1]), 0)
    onehot[...] = jnp.where(lane_count == slot_lane, 1.0, 0.0).astype(jnp.bfloat16)
    in_row = lax.broadcasted_iota(jnp.int32, (all_rows, slots.shape[1]), 0) == slot_row
    for fibre in range(fibres):
        for index in range(2):
            angles[index, fibre : fibre + 1, :] = angle_ref[index, fibre]
    azimuth, elevation = angles[0], angles[1]
    flat = jnp.cos(elevation)
    direction = (jnp.cos(azimuth) * flat, jnp.sin(azimuth) * flat, jnp.sin(elevation))

    for side in range(2):

        @pl.when(y_there[side])
        def _():
            y_copy(1 - side).wait_recv()

        @pl.when(jnp.logical_not(y_there[side]))
        def _():
            y_recv[side] = jnp.zeros(y_recv.shape[1:], jnp.float32)

    for x in range(width):
        for field in range(5):
            fields[x + 1, field, rows - 1 : rows, :] = y_recv[0, field, x : x + 1, :]
            fields[x + 1, field, height : height + 1, :] = y_recv[1, field, x : x + 1, :]
    for side in range(2):

        @pl.when(x_there[side])
        def _():
            x_copy(side).start()

    def await_out(step, carry):
        other = lax.rem(me + step, parts)
        slot_copy(send_out, recv_out, out_send_sems, out_recv_sems, other, other).wait_recv()
        return carry

    lax.fori_loop(1, parts, await_out, 0)

    for field in range(3):
        for part in range(parts):
            for row in range(slot_rows):
                place = field * all_rows + part * slot_rows + row
                picked[place : place + 1, :] = recv_out[
                    part, field : field + 1, row * lanes : (row + 1) * lanes
                ]
    near, rest = halves(picked[...])
    chosen = dot(near, onehot[...]) + dot(rest, onehot[...])
    segments = angles.shape[2]
    for field in range(3):
        piece = chosen[field * all_rows : (field + 1) * all_rows]
        line = jnp.sum(jnp.where(in_row, piece, 0.0), axis=0, keepdims=True)
        for fibre in range(fibres):
            nodes[field, fibre : fibre + 1, :] = line[:, fibre * segments : (fibre + 1) * segments]
    along = jnp.zeros((fibres, segments), jnp.float32)
    for field in range(3):
        place = nodes[field]
        along = along + direction[field] * (pltpu.roll(place, segments - 1, 1) - place)
    live = lax.broadcasted_iota(jnp.int32, along.shape, 1) < segments - 1
    tension = jnp.where(live, stiffness_ref[...] * jnp.maximum(along, 0.0), 0.0)
    terms = []
    for field in range(3):
        pull = tension * direction[field]
        nodes[field] = pull - pltpu.roll(pull, 1, 1)
        line = jnp.concatenate(
            [nodes[field, fibre : fibre + 1, :] for fibre in range(fibres)], axis=1
        )
        terms.append(jnp.where(in_row, line, 0.0))
    near, rest = halves(jnp.concatenate(terms, axis=0))
    picked[...] = dot_t(near, onehot[...]) + dot_t(rest, onehot[...])
    for field in range(3):
        for part in range(parts):
            for row in range(slot_rows):
                place = field * all_rows + part * slot_rows + row
                send_back[part, field : field + 1, row * lanes : (row + 1) * lanes] = picked[
                    place : place + 1, :
                ]

    def give_back(step, carry):
        other = lax.rem(me + step, parts)
        slot_copy(send_back, recv_back, back_send_sems, back_recv_sems, other, me).start()
        return carry

    lax.fori_loop(1, parts, give_back, 0)
    recv_back[me] = send_back[me]

    for side in range(2):
        edge = 0 if side == 0 else width + 1

        @pl.when(x_there[side])
        def _():
            x_copy(1 - side).wait_recv()
            fields[edge] = x_recv[side]

        @pl.when(jnp.logical_not(x_there[side]))
        def _():
            fields[edge] = jnp.zeros(fields.shape[1:], jnp.float32)

    table = mode_stiffness()
    level = lax.broadcasted_iota(jnp.int32, (rows, depth), 1)

    def plane_modes(plane):
        modes = []
        for field in range(3):
            value = fields[plane, field]
            above = jnp.where(level < depth - 1, pltpu.roll(value, depth - 1, 1), 0.0)
            pair = (value + above, above - value)
            beside = [pltpu.roll(item, rows - 1, 0) for item in pair]
            modes.append(
                [pair[0] + beside[0], pair[1] + beside[1], beside[0] - pair[0], beside[1] - pair[1]]
            )
        return modes

    def lift(value):
        return jnp.where(level > 0, pltpu.roll(value, 1, 1), 0.0)

    def layer(plane, carry):
        near_modes, far_modes = plane_modes(plane), plane_modes(plane + 1)
        modes = [None] * 24
        for field in range(3):
            for mode in range(4):
                low_side, high_side = near_modes[field][mode], far_modes[field][mode]
                modes[3 * mode + field] = high_side + low_side
                modes[3 * (mode + 4) + field] = high_side - low_side
        modulus = fields[plane, 3]
        forces = []
        for row in range(24):
            force = None
            for place in range(24):
                if table[row, place] != 0.0:
                    term = jnp.float32(table[row, place]) * modes[place]
                    force = term if force is None else force + term
            forces.append(None if force is None else force * modulus)
        passed = []
        for field in range(3):
            joined = []
            for mode in range(4):
                even, odd = forces[3 * mode + field], forces[3 * (mode + 4) + field]
                even = jnp.zeros_like(odd) if even is None else even
                joined.append(carry[4 * field + mode] + even - odd)
                passed.append(even + odd)
            flat_z = []
            for mode in range(2):
                even, odd = joined[mode], joined[mode + 2]
                flat_z.append(even - odd + pltpu.roll(even + odd, 1, 0))
            result = flat_z[0] - flat_z[1] + lift(flat_z[0] + flat_z[1])
            elastic[plane, field] = result[0:height]
        density = fields[plane, 4]
        density = density + pltpu.roll(density, 1, 0)
        density = density + lift(density)
        mass[plane] = 0.125 * (carry[12] + density)[0:height]
        return tuple(passed) + (density,)

    lax.fori_loop(
        0,
        width + 1,
        layer,
        tuple(jnp.zeros((rows, depth), jnp.float32) for _ in range(13)),
    )

    total[...] = jnp.zeros(total.shape, jnp.float32)

    def spread(step, carry):
        other = lax.rem(me + step, parts)

        @pl.when(other != me)
        def _():
            slot_copy(send_back, recv_back, back_send_sems, back_recv_sems, other, other).wait_recv()

        span = pl.ds(pl.multiple_of(other * cap, lanes), cap)
        force = recv_back[other]
        planar = planar_weights(span)
        near, rest = halves(
            jnp.concatenate([planar * force[field : field + 1] for field in range(3)], axis=0)
        )
        total[...] += dot_t(jnp.concatenate([near, rest], axis=0), weight_z[:, span])
        return carry

    lax.fori_loop(0, parts, spread, 0)
    count = 3 * width * height
    fibre = (
        total[0:count, 0:depth]
        + total[0:count, depth : 2 * depth]
        + total[count : 2 * count, 0:depth]
        + total[count : 2 * count, depth : 2 * depth]
    ).reshape(3, width, height, depth)
    weight = mass[1 : width + 1]
    for field in range(3):
        velocity = velocity_ref[field]
        acceleration = (
            load_ref[field] - elastic[1 : width + 1, field] + fibre[field]
        ) / weight - damping * velocity
        velocity = velocity + time_step * acceleration
        new_velocity_ref[field] = velocity
        new_displacement_ref[field] = displacement_ref[field] + time_step * velocity

    for side in range(2):

        @pl.when(y_there[side])
        def _():
            y_copy(side).wait_send()

        @pl.when(x_there[side])
        def _():
            x_copy(side).wait_send()

    def await_sends(step, carry):
        other = lax.rem(me + step, parts)
        slot_copy(send_out, recv_out, out_send_sems, out_recv_sems, other, me).wait_send()
        slot_copy(send_back, recv_back, back_send_sems, back_recv_sems, other, me).wait_send()
        return carry

    lax.fori_loop(1, parts, await_sends, 0)


def shards(
    displacement,
    velocity,
    load,
    density,
    block_class,
    host_element,
    host_coords,
    fibre_slot,
    fibre_angles,
    fibre_stiffness,
):
    _, width, height, depth = displacement.shape
    parts = lax.axis_size("dom")
    columns = lax.axis_size("blk")
    slots = host_element.shape[1]
    cap = slots // parts
    fibres, _, count = fibre_slot.shape
    rows = height + 8
    f32 = jnp.float32
    vmem = pl.BlockSpec(memory_space=pltpu.VMEM)
    boxes = pltpu.VMEM((parts, 3, cap), f32)
    return pl.pallas_call(
        functools.partial(kernel, parts, columns),
        out_shape=(
            jax.ShapeDtypeStruct(displacement.shape, f32),
            jax.ShapeDtypeStruct(displacement.shape, f32),
        ),
        in_specs=[pl.BlockSpec(memory_space=pltpu.SMEM)] + [vmem] * 9,
        out_specs=(vmem, vmem),
        scratch_shapes=[
            pltpu.VMEM((width + 2, 5, rows, depth), f32),
            pltpu.VMEM((2, 5, width, depth), f32),
            pltpu.VMEM((2, 5, width, depth), f32),
            pltpu.VMEM((2, 5, rows, depth), f32),
            pltpu.VMEM((2 * depth, slots), jnp.bfloat16),
            pltpu.VMEM((width, slots), f32),
            pltpu.VMEM((height, slots), f32),
            pltpu.VMEM((lanes, fibres * count), jnp.bfloat16),
            pltpu.VMEM((2, fibres, count), f32),
            pltpu.VMEM((3 * slots // lanes, lanes), f32),
            pltpu.VMEM((3, fibres, count), f32),
            boxes,
            boxes,
            boxes,
            boxes,
            pltpu.VMEM((6 * width * height, 2 * depth), f32),
            pltpu.VMEM((width + 1, 3, height, depth), f32),
            pltpu.VMEM((width + 1, height, depth), f32),
            pltpu.SemaphoreType.DMA((4,)),
            pltpu.SemaphoreType.DMA((4,)),
            pltpu.SemaphoreType.DMA((parts,)),
            pltpu.SemaphoreType.DMA((parts,)),
            pltpu.SemaphoreType.DMA((parts,)),
            pltpu.SemaphoreType.DMA((parts,)),
        ],
        compiler_params=pltpu.CompilerParams(
            collective_id=0, has_side_effects=True, vmem_limit_bytes=32 * 1024 * 1024
        ),
    )(
        block_class,
        displacement,
        velocity,
        load,
        density,
        host_element,
        host_coords,
        fibre_slot,
        fibre_angles,
        fibre_stiffness,
    )


def solution(mesh):
    return jax.shard_map(
        shards,
        mesh=mesh,
        in_specs=(
            P(None, "dom", "blk", None),
            P(None, "dom", "blk", None),
            P(None, "dom", "blk", None),
            P("dom", "blk", None),
            P("dom", "blk", None),
            P("blk", "dom"),
            P(None, "blk", "dom"),
            P("dom", "blk", None),
            P(None, "dom", "blk", None),
            P("dom", "blk"),
        ),
        out_specs=(P(None, "dom", "blk", None), P(None, "dom", "blk", None)),
        check_vma=False,
    )
```

```python
import functools

import jax
import jax.numpy as jnp
import numpy as np
from jax import lax
from jax.experimental import pallas as pl
from jax.experimental.pallas import tpu as pltpu
from jax.sharding import PartitionSpec as P

class_values = (1.0, 0.45, 0.12)
time_step = 0.25
damping = 0.5
block_edge = 8
lanes = 128
operand_order = (
    "displacement",
    "density",
    "class",
    "element",
    "coords",
    "slot",
    "angle",
    "stiffness",
    "load",
)
MESH = pl.DeviceIdType.MESH


def stiffness_table():
    poisson = 0.3
    lame = poisson / ((1 + poisson) * (1 - 2 * poisson))
    shear = 0.5 / (1 + poisson)
    elastic = np.zeros((6, 6))
    elastic[:3, :3] = lame
    for place in range(3):
        elastic[place, place] += 2 * shear
        elastic[place + 3, place + 3] = shear
    points = [0.5 - 0.5 / np.sqrt(3.0), 0.5 + 0.5 / np.sqrt(3.0)]
    table = np.zeros((24, 24))
    for gauss_r in points:
        for gauss_p in points:
            for gauss_q in points:
                strain = np.zeros((6, 24))
                for corner in range(8):
                    x_bit, y_bit, z_bit = (corner // 4, corner // 2 % 2, corner % 2)
                    along_r = gauss_r if x_bit else 1 - gauss_r
                    along_p = gauss_p if y_bit else 1 - gauss_p
                    along_q = gauss_q if z_bit else 1 - gauss_q
                    d_x = (2 * x_bit - 1) * along_p * along_q
                    d_y = along_r * (2 * y_bit - 1) * along_q
                    d_z = along_r * along_p * (2 * z_bit - 1)
                    column = 3 * corner
                    strain[0, column] = d_x
                    strain[1, column + 1] = d_y
                    strain[2, column + 2] = d_z
                    strain[3, column] = d_y
                    strain[3, column + 1] = d_x
                    strain[4, column + 1] = d_z
                    strain[4, column + 2] = d_y
                    strain[5, column] = d_z
                    strain[5, column + 2] = d_x
                table += 0.125 * strain.T @ elastic @ strain
    return table


def mode_stiffness():
    single = np.linalg.inv(np.array([[1.0, 1.0], [-1.0, 1.0]]))
    back = np.kron(np.kron(np.kron(single, single), single), np.eye(3))
    table = back.T @ stiffness_table() @ back
    return np.where(np.abs(table) < 1e-12, 0.0, table)


def halves(value):
    high = value.astype(jnp.bfloat16)
    low = (value - high.astype(jnp.float32)).astype(jnp.bfloat16)
    return high, low


def quotient(value, divisor):
    if divisor & (divisor - 1) == 0:
        return lax.shift_right_logical(value, jnp.full_like(value, divisor.bit_length() - 1))
    return lax.div(value, jnp.full_like(value, divisor))


def dot(left, right):
    return jnp.dot(left, right, preferred_element_type=jnp.float32)


def dot_t(left, right):
    return lax.dot_general(
        left, right, (((1,), (1,)), ((), ())), preferred_element_type=jnp.float32
    )


def kernel(
    parts,
    columns,
    *refs,
):
    names = len(operand_order)
    sources, ratio_ref, buffers = refs[:names], refs[names], refs[names + 1 :]
    local = dict(zip(operand_order, buffers[:names]))
    step_kernel(parts, columns, sources, local, ratio_ref, *buffers[names:])


def step_kernel(
    parts,
    columns,
    sources,
    local,
    ratio_ref,
    in_sems,
    fields,
    y_send,
    y_recv,
    x_recv,
    weight_z,
    weight_x,
    weight_y,
    onehot,
    angles,
    picked,
    nodes,
    send_out,
    recv_out,
    send_back,
    recv_back,
    total,
    elastic,
    mass,
    y_sems,
    x_sems,
    out_send_sems,
    out_recv_sems,
    back_send_sems,
    back_recv_sems,
):
    copies = {}
    for index, name in enumerate(operand_order):
        copies[name] = pltpu.make_async_copy(sources[index], local[name], in_sems.at[index])
        copies[name].start()
    displacement_ref, load_ref, density_ref = (
        local["displacement"],
        local["load"],
        local["density"],
    )
    class_ref, element_ref, coords_ref = local["class"], local["element"], local["coords"]
    slot_ref, angle_ref, stiffness_ref = local["slot"], local["angle"], local["stiffness"]
    _, width, height, depth = displacement_ref.shape
    rows = fields.shape[2]
    cap = recv_out.shape[2]
    slot_rows = cap // lanes
    all_rows = parts * slot_rows
    fibres = slot_ref.shape[0]
    me = lax.axis_index("dom")
    column = lax.axis_index("blk")

    barrier = pltpu.get_barrier_semaphore()

    def greet(step, carry):
        other = lax.rem(me + step, parts)
        pl.semaphore_signal(barrier, inc=1, device_id=(other, column), device_id_type=MESH)
        return carry

    lax.fori_loop(1, parts, greet, 0)

    @pl.when(column > 0)
    def _():
        pl.semaphore_signal(barrier, inc=1, device_id=(me, column - 1), device_id_type=MESH)

    @pl.when(column < columns - 1)
    def _():
        pl.semaphore_signal(barrier, inc=1, device_id=(me, column + 1), device_id_type=MESH)

    for name in ("displacement", "density", "class"):
        copies[name].wait()

    block_of = quotient(lax.broadcasted_iota(jnp.int32, (1, depth), 1), block_edge)
    for x_block in range(width // block_edge):
        for y_block in range(height // block_edge):
            kinds = class_ref[x_block, y_block : y_block + 1, :]
            classes = jnp.zeros((1, depth), jnp.int32)
            for z_block in range(depth // block_edge):
                classes = jnp.where(block_of == z_block, kinds[:, z_block : z_block + 1], classes)
            factor = jnp.zeros((1, depth), jnp.float32)
            for index, value in enumerate(class_values):
                factor = jnp.where(classes == index, jnp.float32(value), factor)
            span = slice(y_block * block_edge, (y_block + 1) * block_edge)
            for x in range(x_block * block_edge, (x_block + 1) * block_edge):
                density = density_ref[x, span, :]
                fields[x + 1, 3, span, :] = factor * density * density
                fields[x + 1, 4, span, :] = density
    blank = jnp.zeros((rows - height, depth), jnp.float32)
    for x in range(width):
        for field in range(3):
            fields[x + 1, field, 0:height, :] = displacement_ref[field, x]
        for field in range(5):
            fields[x + 1, field, height:rows, :] = blank
    for x in range(width):
        for field in range(5):
            y_send[0, field, x : x + 1, :] = fields[x + 1, field, 0:1, :]
            y_send[1, field, x : x + 1, :] = fields[x + 1, field, height - 1 : height, :]

    for name in ("element", "coords"):
        copies[name].wait()

    def weigh(part, carry):
        span = pl.ds(pl.multiple_of(part * cap, lanes), cap)
        element = element_ref[:, span]
        along_x = quotient(element, height * depth)
        along_y = quotient(element - along_x * (height * depth), depth)
        along_z = element - along_x * (height * depth) - along_y * depth

        def weights(lowest, along, count):
            positions = lax.broadcasted_iota(jnp.int32, (count, cap), 0)
            upper = jnp.where(positions == lowest + 1, along, 0.0)
            return jnp.where(positions == lowest, 1.0 - along, upper)

        weight_x[:, span] = weights(along_x, coords_ref[0, :, span], width)
        weight_y[:, span] = weights(along_y, coords_ref[1, :, span], height)
        high, low = halves(weights(along_z, coords_ref[2, :, span], depth))
        weight_z[0:depth, span] = high
        weight_z[depth : 2 * depth, span] = low
        return carry

    lax.fori_loop(0, parts, weigh, 0)

    def barrier_count():
        return (
            parts
            - 1
            + jnp.where(column > 0, 1, 0)
            + jnp.where(column < columns - 1, 1, 0)
        )

    pl.semaphore_wait(barrier, barrier_count())

    def y_copy(side):
        return pltpu.make_async_remote_copy(
            src_ref=y_send.at[side],
            dst_ref=y_recv.at[1 - side],
            send_sem=y_sems.at[side],
            recv_sem=y_sems.at[3 - side],
            device_id=(me, column - 1 if side == 0 else column + 1),
            device_id_type=MESH,
        )

    def x_copy(side):
        return pltpu.make_async_remote_copy(
            src_ref=fields.at[1 if side == 0 else width],
            dst_ref=x_recv.at[1 - side],
            send_sem=x_sems.at[side],
            recv_sem=x_sems.at[3 - side],
            device_id=(me - 1 if side == 0 else me + 1, column),
            device_id_type=MESH,
        )

    y_there = (column > 0, column < columns - 1)
    x_there = (me > 0, me < parts - 1)
    for side in range(2):

        @pl.when(y_there[side])
        def _():
            y_copy(side).start()

    def slot_copy(source, target, send_sems, recv_sems, other, slot):
        return pltpu.make_async_remote_copy(
            src_ref=source.at[other],
            dst_ref=target.at[slot],
            send_sem=send_sems.at[other],
            recv_sem=recv_sems.at[slot],
            device_id=(other, column),
            device_id_type=MESH,
        )

    high, low = halves(displacement_ref[...].reshape(3 * width * height, depth))
    count = 3 * width * height
    both = jnp.concatenate([high, low], axis=0)
    both = jnp.concatenate([both, both], axis=1)

    def planar_weights(span):
        planar = weight_x[:, span][:, None, :] * weight_y[:, span][None]
        return planar.reshape(width * height, cap)

    def interpolate(step, carry):
        other = lax.rem(me + step, parts)
        span = pl.ds(pl.multiple_of(other * cap, lanes), cap)
        sums = dot(both, weight_z[:, span])
        sums = sums[:count] + sums[count:]
        planar = planar_weights(span)
        for field in range(3):
            piece = sums[field * width * height : (field + 1) * width * height]
            send_out[other, field : field + 1, :] = jnp.sum(piece * planar, axis=0, keepdims=True)

        @pl.when(other != me)
        def _():
            slot_copy(send_out, recv_out, out_send_sems, out_recv_sems, other, me).start()

        return carry

    lax.fori_loop(1, parts + 1, interpolate, 0)
    recv_out[me] = send_out[me]

    for name in ("slot", "angle", "stiffness", "load"):
        copies[name].wait()
    diagonal = lax.broadcasted_iota(jnp.int32, (fibres, fibres), 0) == lax.broadcasted_iota(
        jnp.int32, (fibres, fibres), 1
    )
    stiffness = jnp.sum(jnp.where(diagonal, stiffness_ref[...], 0.0), axis=1, keepdims=True)
    slots = jnp.concatenate([slot_ref[fibre] for fibre in range(fibres)], axis=1)
    slot_row = quotient(slots, lanes)
    slot_lane = slots - slot_row * lanes
    lane_count = lax.broadcasted_iota(jnp.int32, (lanes, slots.shape[1]), 0)
    onehot[...] = jnp.where(lane_count == slot_lane, 1.0, 0.0).astype(jnp.bfloat16)
    in_row = lax.broadcasted_iota(jnp.int32, (all_rows, slots.shape[1]), 0) == slot_row
    for fibre in range(fibres):
        for index in range(2):
            angles[index, fibre : fibre + 1, :] = angle_ref[index, fibre]
    azimuth, elevation = angles[0], angles[1]
    flat = jnp.cos(elevation)
    direction = (jnp.cos(azimuth) * flat, jnp.sin(azimuth) * flat, jnp.sin(elevation))

    for side in range(2):

        @pl.when(y_there[side])
        def _():
            y_copy(1 - side).wait_recv()

        @pl.when(jnp.logical_not(y_there[side]))
        def _():
            y_recv[side] = jnp.zeros(y_recv.shape[1:], jnp.float32)

    for x in range(width):
        for field in range(5):
            fields[x + 1, field, rows - 1 : rows, :] = y_recv[0, field, x : x + 1, :]
            fields[x + 1, field, height : height + 1, :] = y_recv[1, field, x : x + 1, :]
    for side in range(2):

        @pl.when(x_there[side])
        def _():
            x_copy(side).start()

    def await_out(step, carry):
        other = lax.rem(me + step, parts)
        slot_copy(send_out, recv_out, out_send_sems, out_recv_sems, other, other).wait_recv()
        return carry

    lax.fori_loop(1, parts, await_out, 0)

    for field in range(3):
        for part in range(parts):
            for row in range(slot_rows):
                place = field * all_rows + part * slot_rows + row
                picked[place : place + 1, :] = recv_out[
                    part, field : field + 1, row * lanes : (row + 1) * lanes
                ]
    near, rest = halves(picked[...])
    chosen = dot(jnp.concatenate([near, rest], axis=0), onehot[...])
    chosen = chosen[: 3 * all_rows] + chosen[3 * all_rows :]
    segments = angles.shape[2]
    for field in range(3):
        piece = chosen[field * all_rows : (field + 1) * all_rows]
        line = jnp.sum(jnp.where(in_row, piece, 0.0), axis=0, keepdims=True)
        for fibre in range(fibres):
            nodes[field, fibre : fibre + 1, :] = line[:, fibre * segments : (fibre + 1) * segments]
    along = jnp.zeros((fibres, segments), jnp.float32)
    for field in range(3):
        place = nodes[field]
        along = along + direction[field] * (pltpu.roll(place, segments - 1, 1) - place)
    live = lax.broadcasted_iota(jnp.int32, along.shape, 1) < segments - 1
    tension = jnp.where(live, stiffness * jnp.maximum(along, 0.0), 0.0)
    terms = []
    for field in range(3):
        pull = tension * direction[field]
        nodes[field] = pull - pltpu.roll(pull, 1, 1)
        line = jnp.concatenate(
            [nodes[field, fibre : fibre + 1, :] for fibre in range(fibres)], axis=1
        )
        terms.append(jnp.where(in_row, line, 0.0))
    near, rest = halves(jnp.concatenate(terms, axis=0))
    sums = dot_t(jnp.concatenate([near, rest], axis=0), onehot[...])
    picked[...] = sums[: 3 * all_rows] + sums[3 * all_rows :]
    for field in range(3):
        for part in range(parts):
            for row in range(slot_rows):
                place = field * all_rows + part * slot_rows + row
                send_back[part, field : field + 1, row * lanes : (row + 1) * lanes] = picked[
                    place : place + 1, :
                ]

    def give_back(step, carry):
        other = lax.rem(me + step, parts)
        slot_copy(send_back, recv_back, back_send_sems, back_recv_sems, other, me).start()
        return carry

    lax.fori_loop(1, parts, give_back, 0)
    recv_back[me] = send_back[me]

    for side in range(2):
        edge = 0 if side == 0 else width + 1

        @pl.when(x_there[side])
        def _():
            x_copy(1 - side).wait_recv()
            fields[edge] = x_recv[side]

        @pl.when(jnp.logical_not(x_there[side]))
        def _():
            fields[edge] = jnp.zeros(fields.shape[1:], jnp.float32)

    table = mode_stiffness()
    level = lax.broadcasted_iota(jnp.int32, (rows, depth), 1)

    def plane_modes(plane):
        modes = []
        for field in range(3):
            value = fields[plane, field]
            above = jnp.where(level < depth - 1, pltpu.roll(value, depth - 1, 1), 0.0)
            pair = (value + above, above - value)
            beside = [pltpu.roll(item, rows - 1, 0) for item in pair]
            modes.append(
                [pair[0] + beside[0], pair[1] + beside[1], beside[0] - pair[0], beside[1] - pair[1]]
            )
        return modes

    def lift(value):
        return jnp.where(level > 0, pltpu.roll(value, 1, 1), 0.0)

    def layer(plane, carry):
        near_modes, far_modes = plane_modes(plane), plane_modes(plane + 1)
        modes = [None] * 24
        for field in range(3):
            for mode in range(4):
                low_side, high_side = near_modes[field][mode], far_modes[field][mode]
                modes[3 * mode + field] = high_side + low_side
                modes[3 * (mode + 4) + field] = high_side - low_side
        modulus = fields[plane, 3]
        forces = []
        for row in range(24):
            force = None
            for place in range(24):
                if table[row, place] != 0.0:
                    term = jnp.float32(table[row, place]) * modes[place]
                    force = term if force is None else force + term
            forces.append(None if force is None else force * modulus)
        passed = []
        for field in range(3):
            joined = []
            for mode in range(4):
                even, odd = forces[3 * mode + field], forces[3 * (mode + 4) + field]
                even = jnp.zeros_like(odd) if even is None else even
                joined.append(carry[4 * field + mode] + even - odd)
                passed.append(even + odd)
            flat_z = []
            for mode in range(2):
                even, odd = joined[mode], joined[mode + 2]
                flat_z.append(even - odd + pltpu.roll(even + odd, 1, 0))
            result = flat_z[0] - flat_z[1] + lift(flat_z[0] + flat_z[1])
            elastic[plane, field] = result[0:height]
        density = fields[plane, 4]
        density = density + pltpu.roll(density, 1, 0)
        density = density + lift(density)
        mass[plane] = 0.125 * (carry[12] + density)[0:height]
        return tuple(passed) + (density,)

    lax.fori_loop(
        0,
        width + 1,
        layer,
        tuple(jnp.zeros((rows, depth), jnp.float32) for _ in range(13)),
    )

    total[...] = jnp.zeros(total.shape, jnp.float32)

    def spread(step, carry):
        other = lax.rem(me + step, parts)

        @pl.when(other != me)
        def _():
            slot_copy(send_back, recv_back, back_send_sems, back_recv_sems, other, other).wait_recv()

        span = pl.ds(pl.multiple_of(other * cap, lanes), cap)
        force = recv_back[other]
        planar = planar_weights(span)
        near, rest = halves(
            jnp.concatenate([planar * force[field : field + 1] for field in range(3)], axis=0)
        )
        total[...] += dot_t(jnp.concatenate([near, rest], axis=0), weight_z[:, span])
        return carry

    lax.fori_loop(0, parts, spread, 0)
    fibre = (
        total[0:count, 0:depth]
        + total[0:count, depth : 2 * depth]
        + total[count : 2 * count, 0:depth]
        + total[count : 2 * count, depth : 2 * depth]
    ).reshape(3, width, height, depth)
    weight = mass[1 : width + 1]
    for field in range(3):
        ratio_ref[field] = (
            load_ref[field] - elastic[1 : width + 1, field] + fibre[field]
        ) / weight

    for side in range(2):

        @pl.when(y_there[side])
        def _():
            y_copy(side).wait_send()

        @pl.when(x_there[side])
        def _():
            x_copy(side).wait_send()

    def await_sends(step, carry):
        other = lax.rem(me + step, parts)
        slot_copy(send_out, recv_out, out_send_sems, out_recv_sems, other, me).wait_send()
        slot_copy(send_back, recv_back, back_send_sems, back_recv_sems, other, me).wait_send()
        return carry

    lax.fori_loop(1, parts, await_sends, 0)


def shards(
    displacement,
    velocity,
    load,
    density,
    block_class,
    host_element,
    host_coords,
    fibre_slot,
    fibre_angles,
    fibre_stiffness,
):
    _, width, height, depth = displacement.shape
    parts = lax.axis_size("dom")
    columns = lax.axis_size("blk")
    slots = host_element.shape[1]
    cap = slots // parts
    fibres, _, count = fibre_slot.shape
    rows = height + 8
    f32 = jnp.float32
    vmem = pl.BlockSpec(memory_space=pltpu.VMEM)
    boxes = pltpu.VMEM((parts, 3, cap), f32)
    operands = (
        displacement,
        density,
        block_class,
        host_element,
        host_coords,
        fibre_slot,
        fibre_angles,
        fibre_stiffness.reshape(1, fibres),
        load,
    )
    ratio = pl.pallas_call(
        functools.partial(kernel, parts, columns),
        out_shape=jax.ShapeDtypeStruct(displacement.shape, f32),
        in_specs=[pl.BlockSpec(memory_space=pltpu.HBM)] * len(operands),
        out_specs=vmem,
        scratch_shapes=[pltpu.VMEM(operand.shape, operand.dtype) for operand in operands]
        + [
            pltpu.SemaphoreType.DMA((len(operands),)),
            pltpu.VMEM((width + 2, 5, rows, depth), f32),
            pltpu.VMEM((2, 5, width, depth), f32),
            pltpu.VMEM((2, 5, width, depth), f32),
            pltpu.VMEM((2, 5, rows, depth), f32),
            pltpu.VMEM((2 * depth, slots), jnp.bfloat16),
            pltpu.VMEM((width, slots), f32),
            pltpu.VMEM((height, slots), f32),
            pltpu.VMEM((lanes, fibres * count), jnp.bfloat16),
            pltpu.VMEM((2, fibres, count), f32),
            pltpu.VMEM((3 * slots // lanes, lanes), f32),
            pltpu.VMEM((3, fibres, count), f32),
            boxes,
            boxes,
            boxes,
            boxes,
            pltpu.VMEM((6 * width * height, 2 * depth), f32),
            pltpu.VMEM((width + 1, 3, height, depth), f32),
            pltpu.VMEM((width + 1, height, depth), f32),
            pltpu.SemaphoreType.DMA((4,)),
            pltpu.SemaphoreType.DMA((4,)),
            pltpu.SemaphoreType.DMA((parts,)),
            pltpu.SemaphoreType.DMA((parts,)),
            pltpu.SemaphoreType.DMA((parts,)),
            pltpu.SemaphoreType.DMA((parts,)),
        ],
        compiler_params=pltpu.CompilerParams(
            collective_id=0, has_side_effects=True, vmem_limit_bytes=32 * 1024 * 1024
        ),
    )(*operands)
    new_velocity = velocity + time_step * (ratio - damping * velocity)
    return displacement + time_step * new_velocity, new_velocity


def solution(mesh):
    return jax.shard_map(
        shards,
        mesh=mesh,
        in_specs=(
            P(None, "dom", "blk", None),
            P(None, "dom", "blk", None),
            P(None, "dom", "blk", None),
            P("dom", "blk", None),
            P("dom", "blk", None),
            P("blk", "dom"),
            P(None, "blk", "dom"),
            P("dom", "blk", None),
            P(None, "dom", "blk", None),
            P("dom", "blk"),
        ),
        out_specs=(P(None, "dom", "blk", None), P(None, "dom", "blk", None)),
        check_vma=False,
    )
```

```python
import functools

import jax
import jax.numpy as jnp
import numpy as np
from jax import lax
from jax.experimental import pallas as pl
from jax.experimental.pallas import tpu as pltpu
from jax.sharding import PartitionSpec as P

class_values = (1.0, 0.45, 0.12)
time_step = 0.25
damping = 0.5
block_edge = 8
lanes = 128
operand_order = (
    "displacement",
    "density",
    "class",
    "element",
    "coords",
    "slot",
    "angle",
    "stiffness",
    "load",
)
MESH = pl.DeviceIdType.MESH


def stiffness_table():
    poisson = 0.3
    lame = poisson / ((1 + poisson) * (1 - 2 * poisson))
    shear = 0.5 / (1 + poisson)
    elastic = np.zeros((6, 6))
    elastic[:3, :3] = lame
    for place in range(3):
        elastic[place, place] += 2 * shear
        elastic[place + 3, place + 3] = shear
    points = [0.5 - 0.5 / np.sqrt(3.0), 0.5 + 0.5 / np.sqrt(3.0)]
    table = np.zeros((24, 24))
    for gauss_r in points:
        for gauss_p in points:
            for gauss_q in points:
                strain = np.zeros((6, 24))
                for corner in range(8):
                    x_bit, y_bit, z_bit = (corner // 4, corner // 2 % 2, corner % 2)
                    along_r = gauss_r if x_bit else 1 - gauss_r
                    along_p = gauss_p if y_bit else 1 - gauss_p
                    along_q = gauss_q if z_bit else 1 - gauss_q
                    d_x = (2 * x_bit - 1) * along_p * along_q
                    d_y = along_r * (2 * y_bit - 1) * along_q
                    d_z = along_r * along_p * (2 * z_bit - 1)
                    column = 3 * corner
                    strain[0, column] = d_x
                    strain[1, column + 1] = d_y
                    strain[2, column + 2] = d_z
                    strain[3, column] = d_y
                    strain[3, column + 1] = d_x
                    strain[4, column + 1] = d_z
                    strain[4, column + 2] = d_y
                    strain[5, column] = d_z
                    strain[5, column + 2] = d_x
                table += 0.125 * strain.T @ elastic @ strain
    return table


def mode_stiffness():
    single = np.linalg.inv(np.array([[1.0, 1.0], [-1.0, 1.0]]))
    back = np.kron(np.kron(np.kron(single, single), single), np.eye(3))
    table = back.T @ stiffness_table() @ back
    return np.where(np.abs(table) < 1e-12, 0.0, table)


def halves(value):
    high = value.astype(jnp.bfloat16)
    low = (value - high.astype(jnp.float32)).astype(jnp.bfloat16)
    return high, low


def quotient(value, divisor):
    if divisor & (divisor - 1) == 0:
        return lax.shift_right_logical(value, jnp.full_like(value, divisor.bit_length() - 1))
    return lax.div(value, jnp.full_like(value, divisor))


def dot(left, right):
    return jnp.dot(left, right, preferred_element_type=jnp.float32)


def dot_t(left, right):
    return lax.dot_general(
        left, right, (((1,), (1,)), ((), ())), preferred_element_type=jnp.float32
    )


def kernel(
    parts,
    columns,
    *refs,
):
    names = len(operand_order)
    sources, ratio_ref, buffers = refs[:names], refs[names], refs[names + 1 :]
    local = dict(zip(operand_order, buffers[:names]))
    step_kernel(parts, columns, sources, local, ratio_ref, *buffers[names:])


def step_kernel(
    parts,
    columns,
    sources,
    local,
    ratio_ref,
    in_sems,
    fields,
    y_send,
    y_recv,
    x_recv,
    weight_z,
    weight_x,
    weight_y,
    onehot,
    angles,
    picked,
    nodes,
    send_out,
    recv_out,
    send_back,
    recv_back,
    total,
    elastic,
    mass,
    y_sems,
    x_sems,
    out_send_sems,
    out_recv_sems,
    back_send_sems,
    back_recv_sems,
):
    copies = {}
    for index, name in enumerate(operand_order):
        copies[name] = pltpu.make_async_copy(sources[index], local[name], in_sems.at[index])
        copies[name].start()
    displacement_ref, load_ref, density_ref = (
        local["displacement"],
        local["load"],
        local["density"],
    )
    class_ref, element_ref, coords_ref = local["class"], local["element"], local["coords"]
    slot_ref, angle_ref, stiffness_ref = local["slot"], local["angle"], local["stiffness"]
    _, width, height, depth = displacement_ref.shape
    rows = fields.shape[2]
    cap = recv_out.shape[2]
    slot_rows = cap // lanes
    all_rows = parts * slot_rows
    fibres = slot_ref.shape[0]
    me = lax.axis_index("dom")
    column = lax.axis_index("blk")

    barrier = pltpu.get_barrier_semaphore()

    def greet(step, carry):
        other = lax.rem(me + step, parts)
        pl.semaphore_signal(barrier, inc=1, device_id=(other, column), device_id_type=MESH)
        return carry

    lax.fori_loop(1, parts, greet, 0)

    @pl.when(column > 0)
    def _():
        pl.semaphore_signal(barrier, inc=1, device_id=(me, column - 1), device_id_type=MESH)

    @pl.when(column < columns - 1)
    def _():
        pl.semaphore_signal(barrier, inc=1, device_id=(me, column + 1), device_id_type=MESH)

    for name in ("displacement", "density", "class"):
        copies[name].wait()

    block_of = quotient(lax.broadcasted_iota(jnp.int32, (1, depth), 1), block_edge)
    for x_block in range(width // block_edge):
        for y_block in range(height // block_edge):
            kinds = class_ref[x_block, y_block : y_block + 1, :]
            classes = jnp.zeros((1, depth), jnp.int32)
            for z_block in range(depth // block_edge):
                classes = jnp.where(block_of == z_block, kinds[:, z_block : z_block + 1], classes)
            factor = jnp.zeros((1, depth), jnp.float32)
            for index, value in enumerate(class_values):
                factor = jnp.where(classes == index, jnp.float32(value), factor)
            span = slice(y_block * block_edge, (y_block + 1) * block_edge)
            for x in range(x_block * block_edge, (x_block + 1) * block_edge):
                density = density_ref[x, span, :]
                fields[x + 1, 3, span, :] = factor * density * density
                fields[x + 1, 4, span, :] = density
    blank = jnp.zeros((rows - height, depth), jnp.float32)
    for x in range(width):
        for field in range(3):
            fields[x + 1, field, 0:height, :] = displacement_ref[field, x]
        for field in range(5):
            fields[x + 1, field, height:rows, :] = blank
    for x in range(width):
        for field in range(5):
            y_send[0, field, x : x + 1, :] = fields[x + 1, field, 0:1, :]
            y_send[1, field, x : x + 1, :] = fields[x + 1, field, height - 1 : height, :]

    for name in ("element", "coords"):
        copies[name].wait()

    def weigh(part, carry):
        span = pl.ds(pl.multiple_of(part * cap, lanes), cap)
        element = element_ref[:, span]
        along_x = quotient(element, height * depth)
        along_y = quotient(element - along_x * (height * depth), depth)
        along_z = element - along_x * (height * depth) - along_y * depth

        def weights(lowest, along, count):
            positions = lax.broadcasted_iota(jnp.int32, (count, cap), 0)
            upper = jnp.where(positions == lowest + 1, along, 0.0)
            return jnp.where(positions == lowest, 1.0 - along, upper)

        weight_x[:, span] = weights(along_x, coords_ref[0, :, span], width)
        weight_y[:, span] = weights(along_y, coords_ref[1, :, span], height)
        high, low = halves(weights(along_z, coords_ref[2, :, span], depth))
        weight_z[0:depth, span] = high
        weight_z[depth : 2 * depth, span] = low
        return carry

    lax.fori_loop(0, parts, weigh, 0)

    def barrier_count():
        return (
            parts
            - 1
            + jnp.where(column > 0, 1, 0)
            + jnp.where(column < columns - 1, 1, 0)
        )

    pl.semaphore_wait(barrier, barrier_count())

    def y_copy(side):
        return pltpu.make_async_remote_copy(
            src_ref=y_send.at[side],
            dst_ref=y_recv.at[1 - side],
            send_sem=y_sems.at[side],
            recv_sem=y_sems.at[3 - side],
            device_id=(me, column - 1 if side == 0 else column + 1),
            device_id_type=MESH,
        )

    def x_copy(side):
        return pltpu.make_async_remote_copy(
            src_ref=fields.at[1 if side == 0 else width],
            dst_ref=x_recv.at[1 - side],
            send_sem=x_sems.at[side],
            recv_sem=x_sems.at[3 - side],
            device_id=(me - 1 if side == 0 else me + 1, column),
            device_id_type=MESH,
        )

    y_there = (column > 0, column < columns - 1)
    x_there = (me > 0, me < parts - 1)
    for side in range(2):

        @pl.when(y_there[side])
        def _():
            y_copy(side).start()

    def slot_copy(source, target, send_sems, recv_sems, other, slot):
        return pltpu.make_async_remote_copy(
            src_ref=source.at[other],
            dst_ref=target.at[slot],
            send_sem=send_sems.at[other],
            recv_sem=recv_sems.at[slot],
            device_id=(other, column),
            device_id_type=MESH,
        )

    high, low = halves(displacement_ref[...].reshape(3 * width * height, depth))
    count = 3 * width * height
    both = jnp.concatenate([high, low], axis=0)
    both = jnp.concatenate([both, both], axis=1)

    def planar_weights(span):
        planar = weight_x[:, span][:, None, :] * weight_y[:, span][None]
        return planar.reshape(width * height, cap)

    def interpolate(step, carry):
        other = lax.rem(me + step, parts)
        span = pl.ds(pl.multiple_of(other * cap, lanes), cap)
        sums = dot(both, weight_z[:, span])
        sums = sums[:count] + sums[count:]
        planar = planar_weights(span)
        for field in range(3):
            piece = sums[field * width * height : (field + 1) * width * height]
            send_out[other, field : field + 1, :] = jnp.sum(piece * planar, axis=0, keepdims=True)

        @pl.when(other != me)
        def _():
            slot_copy(send_out, recv_out, out_send_sems, out_recv_sems, other, me).start()

        return carry

    lax.fori_loop(1, parts + 1, interpolate, 0)
    recv_out[me] = send_out[me]

    for name in ("slot", "angle", "stiffness", "load"):
        copies[name].wait()
    diagonal = lax.broadcasted_iota(jnp.int32, (fibres, fibres), 0) == lax.broadcasted_iota(
        jnp.int32, (fibres, fibres), 1
    )
    stiffness = jnp.sum(jnp.where(diagonal, stiffness_ref[...], 0.0), axis=1, keepdims=True)
    slots = jnp.concatenate([slot_ref[fibre] for fibre in range(fibres)], axis=1)
    slot_row = quotient(slots, lanes)
    slot_lane = slots - slot_row * lanes
    lane_count = lax.broadcasted_iota(jnp.int32, (lanes, slots.shape[1]), 0)
    onehot[...] = jnp.where(lane_count == slot_lane, 1.0, 0.0).astype(jnp.bfloat16)
    in_row = lax.broadcasted_iota(jnp.int32, (all_rows, slots.shape[1]), 0) == slot_row
    for fibre in range(fibres):
        for index in range(2):
            angles[index, fibre : fibre + 1, :] = angle_ref[index, fibre]
    azimuth, elevation = angles[0], angles[1]
    flat = jnp.cos(elevation)
    direction = (jnp.cos(azimuth) * flat, jnp.sin(azimuth) * flat, jnp.sin(elevation))

    for side in range(2):

        @pl.when(y_there[side])
        def _():
            y_copy(1 - side).wait_recv()

        @pl.when(jnp.logical_not(y_there[side]))
        def _():
            y_recv[side] = jnp.zeros(y_recv.shape[1:], jnp.float32)

    for x in range(width):
        for field in range(5):
            fields[x + 1, field, rows - 1 : rows, :] = y_recv[0, field, x : x + 1, :]
            fields[x + 1, field, height : height + 1, :] = y_recv[1, field, x : x + 1, :]
    for side in range(2):

        @pl.when(x_there[side])
        def _():
            x_copy(side).start()

    def await_out(step, carry):
        other = lax.rem(me + step, parts)
        slot_copy(send_out, recv_out, out_send_sems, out_recv_sems, other, other).wait_recv()
        return carry

    lax.fori_loop(1, parts, await_out, 0)

    for field in range(3):
        for part in range(parts):
            for row in range(slot_rows):
                place = field * all_rows + part * slot_rows + row
                picked[place : place + 1, :] = recv_out[
                    part, field : field + 1, row * lanes : (row + 1) * lanes
                ]
    near, rest = halves(picked[...])
    chosen = dot(jnp.concatenate([near, rest], axis=0), onehot[...])
    chosen = chosen[: 3 * all_rows] + chosen[3 * all_rows :]
    segments = angles.shape[2]
    for field in range(3):
        piece = chosen[field * all_rows : (field + 1) * all_rows]
        line = jnp.sum(jnp.where(in_row, piece, 0.0), axis=0, keepdims=True)
        for fibre in range(fibres):
            nodes[field, fibre : fibre + 1, :] = line[:, fibre * segments : (fibre + 1) * segments]
    along = jnp.zeros((fibres, segments), jnp.float32)
    for field in range(3):
        place = nodes[field]
        along = along + direction[field] * (pltpu.roll(place, segments - 1, 1) - place)
    live = lax.broadcasted_iota(jnp.int32, along.shape, 1) < segments - 1
    tension = jnp.where(live, stiffness * jnp.maximum(along, 0.0), 0.0)
    terms = []
    for field in range(3):
        pull = tension * direction[field]
        nodes[field] = pull - pltpu.roll(pull, 1, 1)
        line = jnp.concatenate(
            [nodes[field, fibre : fibre + 1, :] for fibre in range(fibres)], axis=1
        )
        terms.append(jnp.where(in_row, line, 0.0))
    near, rest = halves(jnp.concatenate(terms, axis=0))
    sums = dot_t(jnp.concatenate([near, rest], axis=0), onehot[...])
    picked[...] = sums[: 3 * all_rows] + sums[3 * all_rows :]
    for field in range(3):
        for part in range(parts):
            for row in range(slot_rows):
                place = field * all_rows + part * slot_rows + row
                send_back[part, field : field + 1, row * lanes : (row + 1) * lanes] = picked[
                    place : place + 1, :
                ]

    def give_back(step, carry):
        other = lax.rem(me + step, parts)
        slot_copy(send_back, recv_back, back_send_sems, back_recv_sems, other, me).start()
        return carry

    lax.fori_loop(1, parts, give_back, 0)
    recv_back[me] = send_back[me]

    for side in range(2):
        edge = 0 if side == 0 else width + 1

        @pl.when(x_there[side])
        def _():
            x_copy(1 - side).wait_recv()
            fields[edge] = x_recv[side]

        @pl.when(jnp.logical_not(x_there[side]))
        def _():
            fields[edge] = jnp.zeros(fields.shape[1:], jnp.float32)

    table = mode_stiffness()
    level = lax.broadcasted_iota(jnp.int32, (rows, depth), 1)

    def plane_modes(plane):
        modes = []
        for field in range(3):
            value = fields[plane, field]
            above = jnp.where(level < depth - 1, pltpu.roll(value, depth - 1, 1), 0.0)
            pair = (value + above, above - value)
            beside = [pltpu.roll(item, rows - 1, 0) for item in pair]
            modes.append(
                [pair[0] + beside[0], pair[1] + beside[1], beside[0] - pair[0], beside[1] - pair[1]]
            )
        return modes

    def lift(value):
        return jnp.where(level > 0, pltpu.roll(value, 1, 1), 0.0)

    def layer(plane, carry):
        near_modes, far_modes = plane_modes(plane), plane_modes(plane + 1)
        modes = [None] * 24
        for field in range(3):
            for mode in range(4):
                low_side, high_side = near_modes[field][mode], far_modes[field][mode]
                modes[3 * mode + field] = high_side + low_side
                modes[3 * (mode + 4) + field] = high_side - low_side
        modulus = fields[plane, 3]
        forces = []
        for row in range(24):
            force = None
            for place in range(24):
                if table[row, place] != 0.0:
                    term = jnp.float32(table[row, place]) * modes[place]
                    force = term if force is None else force + term
            forces.append(None if force is None else force * modulus)
        passed = []
        for field in range(3):
            joined = []
            for mode in range(4):
                even, odd = forces[3 * mode + field], forces[3 * (mode + 4) + field]
                even = jnp.zeros_like(odd) if even is None else even
                joined.append(carry[4 * field + mode] + even - odd)
                passed.append(even + odd)
            flat_z = []
            for mode in range(2):
                even, odd = joined[mode], joined[mode + 2]
                flat_z.append(even - odd + pltpu.roll(even + odd, 1, 0))
            result = flat_z[0] - flat_z[1] + lift(flat_z[0] + flat_z[1])
            elastic[plane, field] = result[0:height]
        density = fields[plane, 4]
        density = density + pltpu.roll(density, 1, 0)
        density = density + lift(density)
        mass[plane] = 0.125 * (carry[12] + density)[0:height]
        return tuple(passed) + (density,)

    lax.fori_loop(
        0,
        width + 1,
        layer,
        tuple(jnp.zeros((rows, depth), jnp.float32) for _ in range(13)),
    )

    total[...] = jnp.zeros(total.shape, jnp.float32)

    def spread(step, carry):
        other = lax.rem(me + step, parts)

        @pl.when(other != me)
        def _():
            slot_copy(send_back, recv_back, back_send_sems, back_recv_sems, other, other).wait_recv()

        span = pl.ds(pl.multiple_of(other * cap, lanes), cap)
        force = recv_back[other]
        planar = planar_weights(span)
        near, rest = halves(
            jnp.concatenate([planar * force[field : field + 1] for field in range(3)], axis=0)
        )
        total[...] += dot_t(jnp.concatenate([near, rest], axis=0), weight_z[:, span])
        return carry

    lax.fori_loop(0, parts, spread, 0)
    fibre = (
        total[0:count, 0:depth]
        + total[0:count, depth : 2 * depth]
        + total[count : 2 * count, 0:depth]
        + total[count : 2 * count, depth : 2 * depth]
    ).reshape(3, width, height, depth)
    weight = mass[1 : width + 1]
    for field in range(3):
        ratio_ref[field] = (
            load_ref[field] - elastic[1 : width + 1, field] + fibre[field]
        ) / weight

    for side in range(2):

        @pl.when(y_there[side])
        def _():
            y_copy(side).wait_send()

        @pl.when(x_there[side])
        def _():
            x_copy(side).wait_send()

    def await_sends(step, carry):
        other = lax.rem(me + step, parts)
        slot_copy(send_out, recv_out, out_send_sems, out_recv_sems, other, me).wait_send()
        slot_copy(send_back, recv_back, back_send_sems, back_recv_sems, other, me).wait_send()
        return carry

    lax.fori_loop(1, parts, await_sends, 0)


def shards(
    displacement,
    velocity,
    load,
    density,
    block_class,
    host_element,
    host_coords,
    fibre_slot,
    fibre_angles,
    fibre_stiffness,
):
    _, width, height, depth = displacement.shape
    parts = lax.axis_size("dom")
    columns = lax.axis_size("blk")
    slots = host_element.shape[1]
    cap = slots // parts
    fibres, _, count = fibre_slot.shape
    rows = height + 8
    f32 = jnp.float32
    vmem = pl.BlockSpec(memory_space=pltpu.VMEM)
    boxes = pltpu.VMEM((parts, 3, cap), f32)
    operands = (
        displacement,
        density,
        block_class,
        host_element,
        host_coords,
        fibre_slot,
        fibre_angles,
        fibre_stiffness.reshape(1, fibres),
        load,
    )
    ratio = pl.pallas_call(
        functools.partial(kernel, parts, columns),
        out_shape=jax.ShapeDtypeStruct(displacement.shape, f32),
        in_specs=[pl.BlockSpec(memory_space=pltpu.HBM)] * len(operands),
        out_specs=vmem,
        scratch_shapes=[pltpu.VMEM(operand.shape, operand.dtype) for operand in operands]
        + [
            pltpu.SemaphoreType.DMA((len(operands),)),
            pltpu.VMEM((width + 2, 5, rows, depth), f32),
            pltpu.VMEM((2, 5, width, depth), f32),
            pltpu.VMEM((2, 5, width, depth), f32),
            pltpu.VMEM((2, 5, rows, depth), f32),
            pltpu.VMEM((2 * depth, slots), jnp.bfloat16),
            pltpu.VMEM((width, slots), f32),
            pltpu.VMEM((height, slots), f32),
            pltpu.VMEM((lanes, fibres * count), jnp.bfloat16),
            pltpu.VMEM((2, fibres, count), f32),
            pltpu.VMEM((3 * slots // lanes, lanes), f32),
            pltpu.VMEM((3, fibres, count), f32),
            boxes,
            boxes,
            boxes,
            boxes,
            pltpu.VMEM((6 * width * height, 2 * depth), f32),
            pltpu.VMEM((width + 1, 3, height, depth), f32),
            pltpu.VMEM((width + 1, height, depth), f32),
            pltpu.SemaphoreType.DMA((4,)),
            pltpu.SemaphoreType.DMA((4,)),
            pltpu.SemaphoreType.DMA((parts,)),
            pltpu.SemaphoreType.DMA((parts,)),
            pltpu.SemaphoreType.DMA((parts,)),
            pltpu.SemaphoreType.DMA((parts,)),
        ],
        compiler_params=pltpu.CompilerParams(
            collective_id=0, has_side_effects=True, vmem_limit_bytes=60 * 1024 * 1024
        ),
    )(*operands)
    new_velocity = velocity + time_step * (ratio - damping * velocity)
    return displacement + time_step * new_velocity, new_velocity


def solution(mesh):
    return jax.shard_map(
        shards,
        mesh=mesh,
        in_specs=(
            P(None, "dom", "blk", None),
            P(None, "dom", "blk", None),
            P(None, "dom", "blk", None),
            P("dom", "blk", None),
            P("dom", "blk", None),
            P("blk", "dom"),
            P(None, "blk", "dom"),
            P("dom", "blk", None),
            P(None, "dom", "blk", None),
            P("dom", "blk"),
        ),
        out_specs=(P(None, "dom", "blk", None), P(None, "dom", "blk", None)),
        check_vma=False,
    )
```

```python
import functools

import jax
import jax.numpy as jnp
import numpy as np
from jax import lax
from jax.experimental import pallas as pl
from jax.experimental.pallas import tpu as pltpu
from jax.sharding import PartitionSpec as P

class_values = (1.0, 0.45, 0.12)
time_step = 0.25
damping = 0.5
block_edge = 8
lanes = 128
operand_order = (
    "displacement",
    "density",
    "class",
    "element",
    "coords",
    "slot",
    "angle",
    "stiffness",
    "load",
)
MESH = pl.DeviceIdType.MESH


def stiffness_table():
    poisson = 0.3
    lame = poisson / ((1 + poisson) * (1 - 2 * poisson))
    shear = 0.5 / (1 + poisson)
    elastic = np.zeros((6, 6))
    elastic[:3, :3] = lame
    for place in range(3):
        elastic[place, place] += 2 * shear
        elastic[place + 3, place + 3] = shear
    points = [0.5 - 0.5 / np.sqrt(3.0), 0.5 + 0.5 / np.sqrt(3.0)]
    table = np.zeros((24, 24))
    for gauss_r in points:
        for gauss_p in points:
            for gauss_q in points:
                strain = np.zeros((6, 24))
                for corner in range(8):
                    x_bit, y_bit, z_bit = (corner // 4, corner // 2 % 2, corner % 2)
                    along_r = gauss_r if x_bit else 1 - gauss_r
                    along_p = gauss_p if y_bit else 1 - gauss_p
                    along_q = gauss_q if z_bit else 1 - gauss_q
                    d_x = (2 * x_bit - 1) * along_p * along_q
                    d_y = along_r * (2 * y_bit - 1) * along_q
                    d_z = along_r * along_p * (2 * z_bit - 1)
                    column = 3 * corner
                    strain[0, column] = d_x
                    strain[1, column + 1] = d_y
                    strain[2, column + 2] = d_z
                    strain[3, column] = d_y
                    strain[3, column + 1] = d_x
                    strain[4, column + 1] = d_z
                    strain[4, column + 2] = d_y
                    strain[5, column] = d_z
                    strain[5, column + 2] = d_x
                table += 0.125 * strain.T @ elastic @ strain
    return table


def mode_stiffness():
    single = np.linalg.inv(np.array([[1.0, 1.0], [-1.0, 1.0]]))
    back = np.kron(np.kron(np.kron(single, single), single), np.eye(3))
    table = back.T @ stiffness_table() @ back
    return np.where(np.abs(table) < 1e-12, 0.0, table)


def halves(value):
    high = value.astype(jnp.bfloat16)
    low = (value - high.astype(jnp.float32)).astype(jnp.bfloat16)
    return high, low


def quotient(value, divisor):
    if divisor & (divisor - 1) == 0:
        return lax.shift_right_logical(value, jnp.full_like(value, divisor.bit_length() - 1))
    return lax.div(value, jnp.full_like(value, divisor))


def dot(left, right):
    return jnp.dot(left, right, preferred_element_type=jnp.float32)


def dot_t(left, right):
    return lax.dot_general(
        left, right, (((1,), (1,)), ((), ())), preferred_element_type=jnp.float32
    )


def kernel(
    parts,
    columns,
    *refs,
):
    names = len(operand_order)
    sources, ratio_ref, buffers = refs[:names], refs[names], refs[names + 1 :]
    local = dict(zip(operand_order, buffers[:names]))
    step_kernel(parts, columns, sources, local, ratio_ref, *buffers[names:])


def step_kernel(
    parts,
    columns,
    sources,
    local,
    ratio_ref,
    in_sems,
    fields,
    y_send,
    y_recv,
    x_recv,
    weight_z,
    weight_x,
    weight_y,
    onehot,
    angles,
    picked,
    nodes,
    send_out,
    recv_out,
    send_back,
    recv_back,
    total,
    elastic,
    mass,
    y_sems,
    x_sems,
    out_send_sems,
    out_recv_sems,
    back_send_sems,
    back_recv_sems,
):
    copies = {}
    for index, name in enumerate(operand_order):
        copies[name] = pltpu.make_async_copy(sources[index], local[name], in_sems.at[index])
        copies[name].start()
    displacement_ref, load_ref, density_ref = (
        local["displacement"],
        local["load"],
        local["density"],
    )
    class_ref, element_ref, coords_ref = local["class"], local["element"], local["coords"]
    slot_ref, angle_ref, stiffness_ref = local["slot"], local["angle"], local["stiffness"]
    _, width, height, depth = displacement_ref.shape
    rows = fields.shape[2]
    cap = recv_out.shape[2]
    slot_rows = cap // lanes
    all_rows = parts * slot_rows
    fibres = slot_ref.shape[0]
    me = lax.axis_index("dom")
    column = lax.axis_index("blk")

    barrier = pltpu.get_barrier_semaphore()

    def greet(step, carry):
        other = lax.rem(me + step, parts)
        pl.semaphore_signal(barrier, inc=1, device_id=(other, column), device_id_type=MESH)
        return carry

    lax.fori_loop(1, parts, greet, 0)

    @pl.when(column > 0)
    def _():
        pl.semaphore_signal(barrier, inc=1, device_id=(me, column - 1), device_id_type=MESH)

    @pl.when(column < columns - 1)
    def _():
        pl.semaphore_signal(barrier, inc=1, device_id=(me, column + 1), device_id_type=MESH)

    for name in ("displacement", "density", "class"):
        copies[name].wait()

    block_of = quotient(lax.broadcasted_iota(jnp.int32, (1, depth), 1), block_edge)
    for x_block in range(width // block_edge):
        for y_block in range(height // block_edge):
            kinds = class_ref[x_block, y_block : y_block + 1, :]
            classes = jnp.zeros((1, depth), jnp.int32)
            for z_block in range(depth // block_edge):
                classes = jnp.where(block_of == z_block, kinds[:, z_block : z_block + 1], classes)
            factor = jnp.zeros((1, depth), jnp.float32)
            for index, value in enumerate(class_values):
                factor = jnp.where(classes == index, jnp.float32(value), factor)
            span = slice(y_block * block_edge, (y_block + 1) * block_edge)
            for x in range(x_block * block_edge, (x_block + 1) * block_edge):
                density = density_ref[x, span, :]
                fields[x + 1, 3, span, :] = factor * density * density
                fields[x + 1, 4, span, :] = density
    blank = jnp.zeros((rows - height, depth), jnp.float32)
    for x in range(width):
        for field in range(3):
            fields[x + 1, field, 0:height, :] = displacement_ref[field, x]
        for field in range(5):
            fields[x + 1, field, height:rows, :] = blank
    for x in range(width):
        for field in range(5):
            y_send[0, field, x : x + 1, :] = fields[x + 1, field, 0:1, :]
            y_send[1, field, x : x + 1, :] = fields[x + 1, field, height - 1 : height, :]

    for name in ("element", "coords"):
        copies[name].wait()

    def weigh(span):
        element = element_ref[:, span]
        along_x = quotient(element, height * depth)
        along_y = quotient(element - along_x * (height * depth), depth)
        along_z = element - along_x * (height * depth) - along_y * depth

        def weights(lowest, along, count):
            positions = lax.broadcasted_iota(jnp.int32, (count, cap), 0)
            upper = jnp.where(positions == lowest + 1, along, 0.0)
            return jnp.where(positions == lowest, 1.0 - along, upper)

        across_x = weights(along_x, coords_ref[0, :, span], width)
        across_y = weights(along_y, coords_ref[1, :, span], height)
        high, low = halves(weights(along_z, coords_ref[2, :, span], depth))
        weight_x[:, span] = across_x
        weight_y[:, span] = across_y
        weight_z[0:depth, span] = high
        weight_z[depth : 2 * depth, span] = low
        planar = (across_x[:, None, :] * across_y[None]).reshape(width * height, cap)
        return planar, jnp.concatenate([high, low], axis=0)

    def barrier_count():
        return (
            parts
            - 1
            + jnp.where(column > 0, 1, 0)
            + jnp.where(column < columns - 1, 1, 0)
        )

    pl.semaphore_wait(barrier, barrier_count())

    def y_copy(side):
        return pltpu.make_async_remote_copy(
            src_ref=y_send.at[side],
            dst_ref=y_recv.at[1 - side],
            send_sem=y_sems.at[side],
            recv_sem=y_sems.at[3 - side],
            device_id=(me, column - 1 if side == 0 else column + 1),
            device_id_type=MESH,
        )

    def x_copy(side):
        return pltpu.make_async_remote_copy(
            src_ref=fields.at[1 if side == 0 else width],
            dst_ref=x_recv.at[1 - side],
            send_sem=x_sems.at[side],
            recv_sem=x_sems.at[3 - side],
            device_id=(me - 1 if side == 0 else me + 1, column),
            device_id_type=MESH,
        )

    y_there = (column > 0, column < columns - 1)
    x_there = (me > 0, me < parts - 1)
    for side in range(2):

        @pl.when(y_there[side])
        def _():
            y_copy(side).start()

    def slot_copy(source, target, send_sems, recv_sems, other, slot):
        return pltpu.make_async_remote_copy(
            src_ref=source.at[other],
            dst_ref=target.at[slot],
            send_sem=send_sems.at[other],
            recv_sem=recv_sems.at[slot],
            device_id=(other, column),
            device_id_type=MESH,
        )

    high, low = halves(displacement_ref[...].reshape(3 * width * height, depth))
    count = 3 * width * height
    both = jnp.concatenate([high, low], axis=0)
    both = jnp.concatenate([both, both], axis=1)

    def planar_weights(span):
        planar = weight_x[:, span][:, None, :] * weight_y[:, span][None]
        return planar.reshape(width * height, cap)

    def interpolate(other):
        span = pl.ds(pl.multiple_of(other * cap, lanes), cap)
        planar, weight = weigh(span)
        sums = dot(both, weight)
        sums = sums[:count] + sums[count:]
        for field in range(3):
            piece = sums[field * width * height : (field + 1) * width * height]
            send_out[other, field : field + 1, :] = jnp.sum(piece * planar, axis=0, keepdims=True)

    def hand_out(step, carry):
        other = lax.rem(me + step, parts)
        interpolate(other)
        slot_copy(send_out, recv_out, out_send_sems, out_recv_sems, other, me).start()
        return carry

    unroll = parts - 1 if parts <= 8 else 1
    lax.fori_loop(1, parts, hand_out, 0, unroll=unroll)
    interpolate(me)
    recv_out[me] = send_out[me]

    for name in ("slot", "angle", "stiffness", "load"):
        copies[name].wait()
    diagonal = lax.broadcasted_iota(jnp.int32, (fibres, fibres), 0) == lax.broadcasted_iota(
        jnp.int32, (fibres, fibres), 1
    )
    stiffness = jnp.sum(jnp.where(diagonal, stiffness_ref[...], 0.0), axis=1, keepdims=True)
    slots = jnp.concatenate([slot_ref[fibre] for fibre in range(fibres)], axis=1)
    slot_row = quotient(slots, lanes)
    slot_lane = slots - slot_row * lanes
    lane_count = lax.broadcasted_iota(jnp.int32, (lanes, slots.shape[1]), 0)
    onehot[...] = jnp.where(lane_count == slot_lane, 1.0, 0.0).astype(jnp.bfloat16)
    in_row = lax.broadcasted_iota(jnp.int32, (all_rows, slots.shape[1]), 0) == slot_row
    for fibre in range(fibres):
        for index in range(2):
            angles[index, fibre : fibre + 1, :] = angle_ref[index, fibre]
    azimuth, elevation = angles[0], angles[1]
    flat = jnp.cos(elevation)
    direction = (jnp.cos(azimuth) * flat, jnp.sin(azimuth) * flat, jnp.sin(elevation))

    for side in range(2):

        @pl.when(y_there[side])
        def _():
            y_copy(1 - side).wait_recv()

        @pl.when(jnp.logical_not(y_there[side]))
        def _():
            y_recv[side] = jnp.zeros(y_recv.shape[1:], jnp.float32)

    for x in range(width):
        for field in range(5):
            fields[x + 1, field, rows - 1 : rows, :] = y_recv[0, field, x : x + 1, :]
            fields[x + 1, field, height : height + 1, :] = y_recv[1, field, x : x + 1, :]
    for side in range(2):

        @pl.when(x_there[side])
        def _():
            x_copy(side).start()

    def await_out(step, carry):
        other = lax.rem(me + step, parts)
        slot_copy(send_out, recv_out, out_send_sems, out_recv_sems, other, other).wait_recv()
        return carry

    lax.fori_loop(1, parts, await_out, 0)

    for field in range(3):
        for part in range(parts):
            for row in range(slot_rows):
                place = field * all_rows + part * slot_rows + row
                picked[place : place + 1, :] = recv_out[
                    part, field : field + 1, row * lanes : (row + 1) * lanes
                ]
    near, rest = halves(picked[...])
    chosen = dot(jnp.concatenate([near, rest], axis=0), onehot[...])
    chosen = chosen[: 3 * all_rows] + chosen[3 * all_rows :]
    segments = angles.shape[2]
    for field in range(3):
        piece = chosen[field * all_rows : (field + 1) * all_rows]
        line = jnp.sum(jnp.where(in_row, piece, 0.0), axis=0, keepdims=True)
        for fibre in range(fibres):
            nodes[field, fibre : fibre + 1, :] = line[:, fibre * segments : (fibre + 1) * segments]
    along = jnp.zeros((fibres, segments), jnp.float32)
    for field in range(3):
        place = nodes[field]
        along = along + direction[field] * (pltpu.roll(place, segments - 1, 1) - place)
    live = lax.broadcasted_iota(jnp.int32, along.shape, 1) < segments - 1
    tension = jnp.where(live, stiffness * jnp.maximum(along, 0.0), 0.0)
    terms = []
    for field in range(3):
        pull = tension * direction[field]
        nodes[field] = pull - pltpu.roll(pull, 1, 1)
        line = jnp.concatenate(
            [nodes[field, fibre : fibre + 1, :] for fibre in range(fibres)], axis=1
        )
        terms.append(jnp.where(in_row, line, 0.0))
    near, rest = halves(jnp.concatenate(terms, axis=0))
    sums = dot_t(jnp.concatenate([near, rest], axis=0), onehot[...])
    picked[...] = sums[: 3 * all_rows] + sums[3 * all_rows :]
    for field in range(3):
        for part in range(parts):
            for row in range(slot_rows):
                place = field * all_rows + part * slot_rows + row
                send_back[part, field : field + 1, row * lanes : (row + 1) * lanes] = picked[
                    place : place + 1, :
                ]

    def give_back(step, carry):
        other = lax.rem(me + step, parts)
        slot_copy(send_back, recv_back, back_send_sems, back_recv_sems, other, me).start()
        return carry

    lax.fori_loop(1, parts, give_back, 0)
    recv_back[me] = send_back[me]

    for side in range(2):
        edge = 0 if side == 0 else width + 1

        @pl.when(x_there[side])
        def _():
            x_copy(1 - side).wait_recv()
            fields[edge] = x_recv[side]

        @pl.when(jnp.logical_not(x_there[side]))
        def _():
            fields[edge] = jnp.zeros(fields.shape[1:], jnp.float32)

    table = mode_stiffness()
    level = lax.broadcasted_iota(jnp.int32, (rows, depth), 1)

    def plane_modes(plane):
        modes = []
        for field in range(3):
            value = fields[plane, field]
            above = jnp.where(level < depth - 1, pltpu.roll(value, depth - 1, 1), 0.0)
            pair = (value + above, above - value)
            beside = [pltpu.roll(item, rows - 1, 0) for item in pair]
            modes.append(
                [pair[0] + beside[0], pair[1] + beside[1], beside[0] - pair[0], beside[1] - pair[1]]
            )
        return modes

    def lift(value):
        return jnp.where(level > 0, pltpu.roll(value, 1, 1), 0.0)

    def layer(plane, carry):
        near_modes, far_modes = plane_modes(plane), plane_modes(plane + 1)
        modes = [None] * 24
        for field in range(3):
            for mode in range(4):
                low_side, high_side = near_modes[field][mode], far_modes[field][mode]
                modes[3 * mode + field] = high_side + low_side
                modes[3 * (mode + 4) + field] = high_side - low_side
        modulus = fields[plane, 3]
        forces = []
        for row in range(24):
            force = None
            for place in range(24):
                if table[row, place] != 0.0:
                    term = jnp.float32(table[row, place]) * modes[place]
                    force = term if force is None else force + term
            forces.append(None if force is None else force * modulus)
        passed = []
        for field in range(3):
            joined = []
            for mode in range(4):
                even, odd = forces[3 * mode + field], forces[3 * (mode + 4) + field]
                even = jnp.zeros_like(odd) if even is None else even
                joined.append(carry[4 * field + mode] + even - odd)
                passed.append(even + odd)
            flat_z = []
            for mode in range(2):
                even, odd = joined[mode], joined[mode + 2]
                flat_z.append(even - odd + pltpu.roll(even + odd, 1, 0))
            result = flat_z[0] - flat_z[1] + lift(flat_z[0] + flat_z[1])
            elastic[plane, field] = result[0:height]
        density = fields[plane, 4]
        density = density + pltpu.roll(density, 1, 0)
        density = density + lift(density)
        mass[plane] = 0.125 * (carry[12] + density)[0:height]
        return tuple(passed) + (density,)

    lax.fori_loop(
        0,
        width + 1,
        layer,
        tuple(jnp.zeros((rows, depth), jnp.float32) for _ in range(13)),
    )


    def spread(other):
        span = pl.ds(pl.multiple_of(other * cap, lanes), cap)
        force = recv_back[other]
        planar = planar_weights(span)
        near, rest = halves(
            jnp.concatenate([planar * force[field : field + 1] for field in range(3)], axis=0)
        )
        return dot_t(jnp.concatenate([near, rest], axis=0), weight_z[:, span])

    def take_back(step, carry):
        other = lax.rem(me + step, parts)
        slot_copy(send_back, recv_back, back_send_sems, back_recv_sems, other, other).wait_recv()
        total[...] += spread(other)
        return carry

    total[...] = spread(me)
    lax.fori_loop(1, parts, take_back, 0, unroll=unroll)
    fibre = (
        total[0:count, 0:depth]
        + total[0:count, depth : 2 * depth]
        + total[count : 2 * count, 0:depth]
        + total[count : 2 * count, depth : 2 * depth]
    ).reshape(3, width, height, depth)
    weight = mass[1 : width + 1]
    for field in range(3):
        ratio_ref[field] = (
            load_ref[field] - elastic[1 : width + 1, field] + fibre[field]
        ) / weight

    for side in range(2):

        @pl.when(y_there[side])
        def _():
            y_copy(side).wait_send()

        @pl.when(x_there[side])
        def _():
            x_copy(side).wait_send()

    def await_sends(step, carry):
        other = lax.rem(me + step, parts)
        slot_copy(send_out, recv_out, out_send_sems, out_recv_sems, other, me).wait_send()
        slot_copy(send_back, recv_back, back_send_sems, back_recv_sems, other, me).wait_send()
        return carry

    lax.fori_loop(1, parts, await_sends, 0)


def shards(
    displacement,
    velocity,
    load,
    density,
    block_class,
    host_element,
    host_coords,
    fibre_slot,
    fibre_angles,
    fibre_stiffness,
):
    _, width, height, depth = displacement.shape
    parts = lax.axis_size("dom")
    columns = lax.axis_size("blk")
    slots = host_element.shape[1]
    cap = slots // parts
    fibres, _, count = fibre_slot.shape
    rows = height + 8
    f32 = jnp.float32
    vmem = pl.BlockSpec(memory_space=pltpu.VMEM)
    boxes = pltpu.VMEM((parts, 3, cap), f32)
    operands = (
        displacement,
        density,
        block_class,
        host_element,
        host_coords,
        fibre_slot,
        fibre_angles,
        fibre_stiffness.reshape(1, fibres),
        load,
    )
    ratio = pl.pallas_call(
        functools.partial(kernel, parts, columns),
        out_shape=jax.ShapeDtypeStruct(displacement.shape, f32),
        in_specs=[pl.BlockSpec(memory_space=pltpu.HBM)] * len(operands),
        out_specs=vmem,
        scratch_shapes=[pltpu.VMEM(operand.shape, operand.dtype) for operand in operands]
        + [
            pltpu.SemaphoreType.DMA((len(operands),)),
            pltpu.VMEM((width + 2, 5, rows, depth), f32),
            pltpu.VMEM((2, 5, width, depth), f32),
            pltpu.VMEM((2, 5, width, depth), f32),
            pltpu.VMEM((2, 5, rows, depth), f32),
            pltpu.VMEM((2 * depth, slots), jnp.bfloat16),
            pltpu.VMEM((width, slots), f32),
            pltpu.VMEM((height, slots), f32),
            pltpu.VMEM((lanes, fibres * count), jnp.bfloat16),
            pltpu.VMEM((2, fibres, count), f32),
            pltpu.VMEM((3 * slots // lanes, lanes), f32),
            pltpu.VMEM((3, fibres, count), f32),
            boxes,
            boxes,
            boxes,
            boxes,
            pltpu.VMEM((6 * width * height, 2 * depth), f32),
            pltpu.VMEM((width + 1, 3, height, depth), f32),
            pltpu.VMEM((width + 1, height, depth), f32),
            pltpu.SemaphoreType.DMA((4,)),
            pltpu.SemaphoreType.DMA((4,)),
            pltpu.SemaphoreType.DMA((parts,)),
            pltpu.SemaphoreType.DMA((parts,)),
            pltpu.SemaphoreType.DMA((parts,)),
            pltpu.SemaphoreType.DMA((parts,)),
        ],
        compiler_params=pltpu.CompilerParams(
            collective_id=0, has_side_effects=True, vmem_limit_bytes=60 * 1024 * 1024
        ),
    )(*operands)
    new_velocity = velocity + time_step * (ratio - damping * velocity)
    return displacement + time_step * new_velocity, new_velocity


def solution(mesh):
    return jax.shard_map(
        shards,
        mesh=mesh,
        in_specs=(
            P(None, "dom", "blk", None),
            P(None, "dom", "blk", None),
            P(None, "dom", "blk", None),
            P("dom", "blk", None),
            P("dom", "blk", None),
            P("blk", "dom"),
            P(None, "blk", "dom"),
            P("dom", "blk", None),
            P(None, "dom", "blk", None),
            P("dom", "blk"),
        ),
        out_specs=(P(None, "dom", "blk", None), P(None, "dom", "blk", None)),
        check_vma=False,
    )
```

```python
import functools

import jax
import jax.numpy as jnp
import numpy as np
from jax import lax
from jax.experimental import pallas as pl
from jax.experimental.pallas import tpu as pltpu
from jax.sharding import PartitionSpec as P

class_values = (1.0, 0.45, 0.12)
time_step = 0.25
damping = 0.5
block_edge = 8
lanes = 128
operand_order = (
    "displacement",
    "density",
    "class",
    "element",
    "coords",
    "slot",
    "angle",
    "stiffness",
    "load",
)
MESH = pl.DeviceIdType.MESH


def stiffness_table():
    poisson = 0.3
    lame = poisson / ((1 + poisson) * (1 - 2 * poisson))
    shear = 0.5 / (1 + poisson)
    elastic = np.zeros((6, 6))
    elastic[:3, :3] = lame
    for place in range(3):
        elastic[place, place] += 2 * shear
        elastic[place + 3, place + 3] = shear
    points = [0.5 - 0.5 / np.sqrt(3.0), 0.5 + 0.5 / np.sqrt(3.0)]
    table = np.zeros((24, 24))
    for gauss_r in points:
        for gauss_p in points:
            for gauss_q in points:
                strain = np.zeros((6, 24))
                for corner in range(8):
                    x_bit, y_bit, z_bit = (corner // 4, corner // 2 % 2, corner % 2)
                    along_r = gauss_r if x_bit else 1 - gauss_r
                    along_p = gauss_p if y_bit else 1 - gauss_p
                    along_q = gauss_q if z_bit else 1 - gauss_q
                    d_x = (2 * x_bit - 1) * along_p * along_q
                    d_y = along_r * (2 * y_bit - 1) * along_q
                    d_z = along_r * along_p * (2 * z_bit - 1)
                    column = 3 * corner
                    strain[0, column] = d_x
                    strain[1, column + 1] = d_y
                    strain[2, column + 2] = d_z
                    strain[3, column] = d_y
                    strain[3, column + 1] = d_x
                    strain[4, column + 1] = d_z
                    strain[4, column + 2] = d_y
                    strain[5, column] = d_z
                    strain[5, column + 2] = d_x
                table += 0.125 * strain.T @ elastic @ strain
    return table


def mode_stiffness():
    single = np.linalg.inv(np.array([[1.0, 1.0], [-1.0, 1.0]]))
    back = np.kron(np.kron(np.kron(single, single), single), np.eye(3))
    table = back.T @ stiffness_table() @ back
    return np.where(np.abs(table) < 1e-12, 0.0, table)


def halves(value):
    high = value.astype(jnp.bfloat16)
    low = (value - high.astype(jnp.float32)).astype(jnp.bfloat16)
    return high, low


def quotient(value, divisor):
    if divisor & (divisor - 1) == 0:
        return lax.shift_right_logical(value, jnp.full_like(value, divisor.bit_length() - 1))
    return lax.div(value, jnp.full_like(value, divisor))


def dot(left, right):
    return jnp.dot(left, right, preferred_element_type=jnp.float32)


def dot_t(left, right):
    return lax.dot_general(
        left, right, (((1,), (1,)), ((), ())), preferred_element_type=jnp.float32
    )


def kernel(
    parts,
    columns,
    *refs,
):
    names = len(operand_order)
    sources, ratio_ref, buffers = refs[:names], refs[names], refs[names + 1 :]
    local = dict(zip(operand_order, buffers[:names]))
    step_kernel(parts, columns, sources, local, ratio_ref, *buffers[names:])


def step_kernel(
    parts,
    columns,
    sources,
    local,
    ratio_ref,
    in_sems,
    fields,
    y_send,
    y_recv,
    x_recv,
    weight_z,
    weight_x,
    weight_y,
    onehot,
    angles,
    picked,
    nodes,
    send_out,
    recv_out,
    send_back,
    recv_back,
    total,
    elastic,
    mass,
    y_sems,
    x_sems,
    out_send_sems,
    out_recv_sems,
    back_send_sems,
    back_recv_sems,
):
    copies = {}
    for index, name in enumerate(operand_order):
        copies[name] = pltpu.make_async_copy(sources[index], local[name], in_sems.at[index])
        copies[name].start()
    displacement_ref, load_ref, density_ref = (
        local["displacement"],
        local["load"],
        local["density"],
    )
    class_ref, element_ref, coords_ref = local["class"], local["element"], local["coords"]
    slot_ref, angle_ref, stiffness_ref = local["slot"], local["angle"], local["stiffness"]
    _, width, height, depth = displacement_ref.shape
    rows = fields.shape[2]
    cap = recv_out.shape[2]
    slot_rows = cap // lanes
    all_rows = parts * slot_rows
    fibres = slot_ref.shape[0]
    me = lax.axis_index("dom")
    column = lax.axis_index("blk")

    barrier = pltpu.get_barrier_semaphore()

    def greet(step, carry):
        other = lax.rem(me + step, parts)
        pl.semaphore_signal(barrier, inc=1, device_id=(other, column), device_id_type=MESH)
        return carry

    lax.fori_loop(1, parts, greet, 0)

    @pl.when(column > 0)
    def _():
        pl.semaphore_signal(barrier, inc=1, device_id=(me, column - 1), device_id_type=MESH)

    @pl.when(column < columns - 1)
    def _():
        pl.semaphore_signal(barrier, inc=1, device_id=(me, column + 1), device_id_type=MESH)

    for name in ("displacement", "density", "class"):
        copies[name].wait()

    block_of = quotient(lax.broadcasted_iota(jnp.int32, (1, depth), 1), block_edge)
    for x_block in range(width // block_edge):
        for y_block in range(height // block_edge):
            kinds = class_ref[x_block, y_block : y_block + 1, :]
            classes = jnp.zeros((1, depth), jnp.int32)
            for z_block in range(depth // block_edge):
                classes = jnp.where(block_of == z_block, kinds[:, z_block : z_block + 1], classes)
            factor = jnp.zeros((1, depth), jnp.float32)
            for index, value in enumerate(class_values):
                factor = jnp.where(classes == index, jnp.float32(value), factor)
            span = slice(y_block * block_edge, (y_block + 1) * block_edge)
            for x in range(x_block * block_edge, (x_block + 1) * block_edge):
                density = density_ref[x, span, :]
                fields[x + 1, 3, span, :] = factor * density * density
                fields[x + 1, 4, span, :] = density
    blank = jnp.zeros((rows - height, depth), jnp.float32)
    for x in range(width):
        for field in range(3):
            fields[x + 1, field, 0:height, :] = displacement_ref[field, x]
        for field in range(5):
            fields[x + 1, field, height:rows, :] = blank
    for x in range(width):
        for field in range(5):
            y_send[0, field, x : x + 1, :] = fields[x + 1, field, 0:1, :]
            y_send[1, field, x : x + 1, :] = fields[x + 1, field, height - 1 : height, :]

    for name in ("element", "coords"):
        copies[name].wait()

    def weigh(part, carry):
        span = pl.ds(pl.multiple_of(part * cap, lanes), cap)
        element = element_ref[:, span]
        along_x = quotient(element, height * depth)
        along_y = quotient(element - along_x * (height * depth), depth)
        along_z = element - along_x * (height * depth) - along_y * depth

        def weights(lowest, along, count):
            positions = lax.broadcasted_iota(jnp.int32, (count, cap), 0)
            upper = jnp.where(positions == lowest + 1, along, 0.0)
            return jnp.where(positions == lowest, 1.0 - along, upper)

        weight_x[:, span] = weights(along_x, coords_ref[0, :, span], width)
        weight_y[:, span] = weights(along_y, coords_ref[1, :, span], height)
        high, low = halves(weights(along_z, coords_ref[2, :, span], depth))
        weight_z[0:depth, span] = high
        weight_z[depth : 2 * depth, span] = low
        return carry

    lax.fori_loop(0, parts, weigh, 0)

    def barrier_count():
        return (
            parts
            - 1
            + jnp.where(column > 0, 1, 0)
            + jnp.where(column < columns - 1, 1, 0)
        )

    pl.semaphore_wait(barrier, barrier_count())

    def y_copy(side):
        return pltpu.make_async_remote_copy(
            src_ref=y_send.at[side],
            dst_ref=y_recv.at[1 - side],
            send_sem=y_sems.at[side],
            recv_sem=y_sems.at[3 - side],
            device_id=(me, column - 1 if side == 0 else column + 1),
            device_id_type=MESH,
        )

    def x_copy(side):
        return pltpu.make_async_remote_copy(
            src_ref=fields.at[1 if side == 0 else width],
            dst_ref=x_recv.at[1 - side],
            send_sem=x_sems.at[side],
            recv_sem=x_sems.at[3 - side],
            device_id=(me - 1 if side == 0 else me + 1, column),
            device_id_type=MESH,
        )

    y_there = (column > 0, column < columns - 1)
    x_there = (me > 0, me < parts - 1)
    for side in range(2):

        @pl.when(y_there[side])
        def _():
            y_copy(side).start()

    def slot_copy(source, target, send_sems, recv_sems, other, slot):
        return pltpu.make_async_remote_copy(
            src_ref=source.at[other],
            dst_ref=target.at[slot],
            send_sem=send_sems.at[other],
            recv_sem=recv_sems.at[slot],
            device_id=(other, column),
            device_id_type=MESH,
        )

    high, low = halves(displacement_ref[...].reshape(3 * width * height, depth))
    count = 3 * width * height
    both = jnp.concatenate([high, low], axis=0)
    both = jnp.concatenate([both, both], axis=1)

    def planar_weights(span):
        planar = weight_x[:, span][:, None, :] * weight_y[:, span][None]
        return planar.reshape(width * height, cap)

    def interpolate(step, carry):
        other = lax.rem(me + step, parts)
        span = pl.ds(pl.multiple_of(other * cap, lanes), cap)
        sums = dot(both, weight_z[:, span])
        sums = sums[:count] + sums[count:]
        planar = planar_weights(span)
        for field in range(3):
            piece = sums[field * width * height : (field + 1) * width * height]
            send_out[other, field : field + 1, :] = jnp.sum(piece * planar, axis=0, keepdims=True)

        @pl.when(other != me)
        def _():
            slot_copy(send_out, recv_out, out_send_sems, out_recv_sems, other, me).start()

        return carry

    lax.fori_loop(1, parts + 1, interpolate, 0)
    recv_out[me] = send_out[me]

    for name in ("slot", "angle", "stiffness", "load"):
        copies[name].wait()
    diagonal = lax.broadcasted_iota(jnp.int32, (fibres, fibres), 0) == lax.broadcasted_iota(
        jnp.int32, (fibres, fibres), 1
    )
    stiffness = jnp.sum(jnp.where(diagonal, stiffness_ref[...], 0.0), axis=1, keepdims=True)
    slots = jnp.concatenate([slot_ref[fibre] for fibre in range(fibres)], axis=1)
    slot_row = quotient(slots, lanes)
    slot_lane = slots - slot_row * lanes
    lane_count = lax.broadcasted_iota(jnp.int32, (lanes, slots.shape[1]), 0)
    onehot[...] = jnp.where(lane_count == slot_lane, 1.0, 0.0).astype(jnp.bfloat16)
    in_row = lax.broadcasted_iota(jnp.int32, (all_rows, slots.shape[1]), 0) == slot_row
    for fibre in range(fibres):
        for index in range(2):
            angles[index, fibre : fibre + 1, :] = angle_ref[index, fibre]
    azimuth, elevation = angles[0], angles[1]
    flat = jnp.cos(elevation)
    direction = (jnp.cos(azimuth) * flat, jnp.sin(azimuth) * flat, jnp.sin(elevation))

    for side in range(2):

        @pl.when(y_there[side])
        def _():
            y_copy(1 - side).wait_recv()

        @pl.when(jnp.logical_not(y_there[side]))
        def _():
            y_recv[side] = jnp.zeros(y_recv.shape[1:], jnp.float32)

    for x in range(width):
        for field in range(5):
            fields[x + 1, field, rows - 1 : rows, :] = y_recv[0, field, x : x + 1, :]
            fields[x + 1, field, height : height + 1, :] = y_recv[1, field, x : x + 1, :]
    for side in range(2):

        @pl.when(x_there[side])
        def _():
            x_copy(side).start()

    def await_out(step, carry):
        other = lax.rem(me + step, parts)
        slot_copy(send_out, recv_out, out_send_sems, out_recv_sems, other, other).wait_recv()
        return carry

    lax.fori_loop(1, parts, await_out, 0)

    for field in range(3):
        for part in range(parts):
            for row in range(slot_rows):
                place = field * all_rows + part * slot_rows + row
                picked[place : place + 1, :] = recv_out[
                    part, field : field + 1, row * lanes : (row + 1) * lanes
                ]
    near, rest = halves(picked[...])
    chosen = dot(jnp.concatenate([near, rest], axis=0), onehot[...])
    chosen = chosen[: 3 * all_rows] + chosen[3 * all_rows :]
    segments = angles.shape[2]
    for field in range(3):
        piece = chosen[field * all_rows : (field + 1) * all_rows]
        line = jnp.sum(jnp.where(in_row, piece, 0.0), axis=0, keepdims=True)
        for fibre in range(fibres):
            nodes[field, fibre : fibre + 1, :] = line[:, fibre * segments : (fibre + 1) * segments]
    along = jnp.zeros((fibres, segments), jnp.float32)
    for field in range(3):
        place = nodes[field]
        along = along + direction[field] * (pltpu.roll(place, segments - 1, 1) - place)
    live = lax.broadcasted_iota(jnp.int32, along.shape, 1) < segments - 1
    tension = jnp.where(live, stiffness * jnp.maximum(along, 0.0), 0.0)
    terms = []
    for field in range(3):
        pull = tension * direction[field]
        nodes[field] = pull - pltpu.roll(pull, 1, 1)
        line = jnp.concatenate(
            [nodes[field, fibre : fibre + 1, :] for fibre in range(fibres)], axis=1
        )
        terms.append(jnp.where(in_row, line, 0.0))
    near, rest = halves(jnp.concatenate(terms, axis=0))
    sums = dot_t(jnp.concatenate([near, rest], axis=0), onehot[...])
    picked[...] = sums[: 3 * all_rows] + sums[3 * all_rows :]
    for field in range(3):
        for part in range(parts):
            for row in range(slot_rows):
                place = field * all_rows + part * slot_rows + row
                send_back[part, field : field + 1, row * lanes : (row + 1) * lanes] = picked[
                    place : place + 1, :
                ]

    def give_back(step, carry):
        other = lax.rem(me + step, parts)
        slot_copy(send_back, recv_back, back_send_sems, back_recv_sems, other, me).start()
        return carry

    lax.fori_loop(1, parts, give_back, 0)
    recv_back[me] = send_back[me]

    for side in range(2):
        edge = 0 if side == 0 else width + 1

        @pl.when(x_there[side])
        def _():
            x_copy(1 - side).wait_recv()
            fields[edge] = x_recv[side]

        @pl.when(jnp.logical_not(x_there[side]))
        def _():
            fields[edge] = jnp.zeros(fields.shape[1:], jnp.float32)

    table = mode_stiffness()
    level = lax.broadcasted_iota(jnp.int32, (rows, depth), 1)

    def plane_modes(plane):
        modes = []
        for field in range(3):
            value = fields[plane, field]
            above = jnp.where(level < depth - 1, pltpu.roll(value, depth - 1, 1), 0.0)
            pair = (value + above, above - value)
            beside = [pltpu.roll(item, rows - 1, 0) for item in pair]
            modes.append(
                [pair[0] + beside[0], pair[1] + beside[1], beside[0] - pair[0], beside[1] - pair[1]]
            )
        return modes

    def lift(value):
        return jnp.where(level > 0, pltpu.roll(value, 1, 1), 0.0)

    def layer(plane, carry):
        near_modes, far_modes = plane_modes(plane), plane_modes(plane + 1)
        modes = [None] * 24
        for field in range(3):
            for mode in range(4):
                low_side, high_side = near_modes[field][mode], far_modes[field][mode]
                modes[3 * mode + field] = high_side + low_side
                modes[3 * (mode + 4) + field] = high_side - low_side
        modulus = fields[plane, 3]
        forces = []
        for row in range(24):
            force = None
            for place in range(24):
                if table[row, place] != 0.0:
                    term = jnp.float32(table[row, place]) * modes[place]
                    force = term if force is None else force + term
            forces.append(None if force is None else force * modulus)
        passed = []
        for field in range(3):
            joined = []
            for mode in range(4):
                even, odd = forces[3 * mode + field], forces[3 * (mode + 4) + field]
                even = jnp.zeros_like(odd) if even is None else even
                joined.append(carry[4 * field + mode] + even - odd)
                passed.append(even + odd)
            flat_z = []
            for mode in range(2):
                even, odd = joined[mode], joined[mode + 2]
                flat_z.append(even - odd + pltpu.roll(even + odd, 1, 0))
            result = flat_z[0] - flat_z[1] + lift(flat_z[0] + flat_z[1])
            elastic[plane, field] = result[0:height]
        density = fields[plane, 4]
        density = density + pltpu.roll(density, 1, 0)
        density = density + lift(density)
        mass[plane] = 0.125 * (carry[12] + density)[0:height]
        return tuple(passed) + (density,)

    lax.fori_loop(
        0,
        width + 1,
        layer,
        tuple(jnp.zeros((rows, depth), jnp.float32) for _ in range(13)),
    )

    total[...] = jnp.zeros(total.shape, jnp.float32)

    def spread(step, carry):
        other = lax.rem(me + step, parts)

        @pl.when(other != me)
        def _():
            slot_copy(send_back, recv_back, back_send_sems, back_recv_sems, other, other).wait_recv()

        span = pl.ds(pl.multiple_of(other * cap, lanes), cap)
        force = recv_back[other]
        planar = planar_weights(span)
        near, rest = halves(
            jnp.concatenate([planar * force[field : field + 1] for field in range(3)], axis=0)
        )
        total[...] += dot_t(jnp.concatenate([near, rest], axis=0), weight_z[:, span])
        return carry

    lax.fori_loop(0, parts, spread, 0)
    fibre = (
        total[0:count, 0:depth]
        + total[0:count, depth : 2 * depth]
        + total[count : 2 * count, 0:depth]
        + total[count : 2 * count, depth : 2 * depth]
    ).reshape(3, width, height, depth)
    weight = mass[1 : width + 1]
    for field in range(3):
        ratio_ref[field] = (
            load_ref[field] - elastic[1 : width + 1, field] + fibre[field]
        ) / weight

    for side in range(2):

        @pl.when(y_there[side])
        def _():
            y_copy(side).wait_send()

        @pl.when(x_there[side])
        def _():
            x_copy(side).wait_send()

    def await_sends(step, carry):
        other = lax.rem(me + step, parts)
        slot_copy(send_out, recv_out, out_send_sems, out_recv_sems, other, me).wait_send()
        slot_copy(send_back, recv_back, back_send_sems, back_recv_sems, other, me).wait_send()
        return carry

    lax.fori_loop(1, parts, await_sends, 0)


def shards(
    displacement,
    velocity,
    load,
    density,
    block_class,
    host_element,
    host_coords,
    fibre_slot,
    fibre_angles,
    fibre_stiffness,
):
    _, width, height, depth = displacement.shape
    parts = lax.axis_size("dom")
    columns = lax.axis_size("blk")
    slots = host_element.shape[1]
    cap = slots // parts
    fibres, _, count = fibre_slot.shape
    rows = height + 8
    f32 = jnp.float32
    vmem = pl.BlockSpec(memory_space=pltpu.VMEM)
    boxes = pltpu.VMEM((parts, 3, cap), f32)
    operands = (
        displacement,
        density,
        block_class,
        host_element,
        host_coords,
        fibre_slot,
        fibre_angles,
        fibre_stiffness.reshape(1, fibres),
        load,
    )
    ratio = pl.pallas_call(
        functools.partial(kernel, parts, columns),
        out_shape=pltpu.VMEM(displacement.shape, f32),
        in_specs=[pl.BlockSpec(memory_space=pltpu.HBM)] * len(operands),
        out_specs=vmem,
        scratch_shapes=[pltpu.VMEM(operand.shape, operand.dtype) for operand in operands]
        + [
            pltpu.SemaphoreType.DMA((len(operands),)),
            pltpu.VMEM((width + 2, 5, rows, depth), f32),
            pltpu.VMEM((2, 5, width, depth), f32),
            pltpu.VMEM((2, 5, width, depth), f32),
            pltpu.VMEM((2, 5, rows, depth), f32),
            pltpu.VMEM((2 * depth, slots), jnp.bfloat16),
            pltpu.VMEM((width, slots), f32),
            pltpu.VMEM((height, slots), f32),
            pltpu.VMEM((lanes, fibres * count), jnp.bfloat16),
            pltpu.VMEM((2, fibres, count), f32),
            pltpu.VMEM((3 * slots // lanes, lanes), f32),
            pltpu.VMEM((3, fibres, count), f32),
            boxes,
            boxes,
            boxes,
            boxes,
            pltpu.VMEM((6 * width * height, 2 * depth), f32),
            pltpu.VMEM((width + 1, 3, height, depth), f32),
            pltpu.VMEM((width + 1, height, depth), f32),
            pltpu.SemaphoreType.DMA((4,)),
            pltpu.SemaphoreType.DMA((4,)),
            pltpu.SemaphoreType.DMA((parts,)),
            pltpu.SemaphoreType.DMA((parts,)),
            pltpu.SemaphoreType.DMA((parts,)),
            pltpu.SemaphoreType.DMA((parts,)),
        ],
        compiler_params=pltpu.CompilerParams(
            collective_id=0, has_side_effects=True, vmem_limit_bytes=60 * 1024 * 1024
        ),
    )(*operands)
    new_velocity = velocity + time_step * (ratio - damping * velocity)
    return displacement + time_step * new_velocity, new_velocity


def solution(mesh):
    return jax.shard_map(
        shards,
        mesh=mesh,
        in_specs=(
            P(None, "dom", "blk", None),
            P(None, "dom", "blk", None),
            P(None, "dom", "blk", None),
            P("dom", "blk", None),
            P("dom", "blk", None),
            P("blk", "dom"),
            P(None, "blk", "dom"),
            P("dom", "blk", None),
            P(None, "dom", "blk", None),
            P("dom", "blk"),
        ),
        out_specs=(P(None, "dom", "blk", None), P(None, "dom", "blk", None)),
        check_vma=False,
    )
```

```python
import functools

import jax
import jax.numpy as jnp
import numpy as np
from jax import lax
from jax.experimental import pallas as pl
from jax.experimental.pallas import tpu as pltpu
from jax.sharding import PartitionSpec as P

class_values = (1.0, 0.45, 0.12)
time_step = 0.25
damping = 0.5
block_edge = 8
lanes = 128
operand_order = (
    "displacement",
    "density",
    "class",
    "element",
    "coords",
    "slot",
    "angle",
    "stiffness",
    "load",
)
MESH = pl.DeviceIdType.MESH


def stiffness_table():
    poisson = 0.3
    lame = poisson / ((1 + poisson) * (1 - 2 * poisson))
    shear = 0.5 / (1 + poisson)
    elastic = np.zeros((6, 6))
    elastic[:3, :3] = lame
    for place in range(3):
        elastic[place, place] += 2 * shear
        elastic[place + 3, place + 3] = shear
    points = [0.5 - 0.5 / np.sqrt(3.0), 0.5 + 0.5 / np.sqrt(3.0)]
    table = np.zeros((24, 24))
    for gauss_r in points:
        for gauss_p in points:
            for gauss_q in points:
                strain = np.zeros((6, 24))
                for corner in range(8):
                    x_bit, y_bit, z_bit = (corner // 4, corner // 2 % 2, corner % 2)
                    along_r = gauss_r if x_bit else 1 - gauss_r
                    along_p = gauss_p if y_bit else 1 - gauss_p
                    along_q = gauss_q if z_bit else 1 - gauss_q
                    d_x = (2 * x_bit - 1) * along_p * along_q
                    d_y = along_r * (2 * y_bit - 1) * along_q
                    d_z = along_r * along_p * (2 * z_bit - 1)
                    column = 3 * corner
                    strain[0, column] = d_x
                    strain[1, column + 1] = d_y
                    strain[2, column + 2] = d_z
                    strain[3, column] = d_y
                    strain[3, column + 1] = d_x
                    strain[4, column + 1] = d_z
                    strain[4, column + 2] = d_y
                    strain[5, column] = d_z
                    strain[5, column + 2] = d_x
                table += 0.125 * strain.T @ elastic @ strain
    return table


def mode_stiffness():
    single = np.linalg.inv(np.array([[1.0, 1.0], [-1.0, 1.0]]))
    back = np.kron(np.kron(np.kron(single, single), single), np.eye(3))
    table = back.T @ stiffness_table() @ back
    return np.where(np.abs(table) < 1e-12, 0.0, table)


def halves(value):
    high = value.astype(jnp.bfloat16)
    low = (value - high.astype(jnp.float32)).astype(jnp.bfloat16)
    return high, low


def quotient(value, divisor):
    if divisor & (divisor - 1) == 0:
        return lax.shift_right_logical(value, jnp.full_like(value, divisor.bit_length() - 1))
    return lax.div(value, jnp.full_like(value, divisor))


def dot(left, right):
    return jnp.dot(left, right, preferred_element_type=jnp.float32)


def dot_t(left, right):
    return lax.dot_general(
        left, right, (((1,), (1,)), ((), ())), preferred_element_type=jnp.float32
    )


def kernel(
    parts,
    columns,
    *refs,
):
    names = len(operand_order)
    sources, ratio_ref, buffers = refs[:names], refs[names], refs[names + 1 :]
    local = dict(zip(operand_order, buffers[:names]))
    step_kernel(parts, columns, sources, local, ratio_ref, *buffers[names:])


def step_kernel(
    parts,
    columns,
    sources,
    local,
    ratio_ref,
    in_sems,
    fields,
    y_send,
    y_recv,
    x_recv,
    weight_z,
    weight_x,
    weight_y,
    onehot,
    angles,
    picked,
    nodes,
    send_out,
    recv_out,
    send_back,
    recv_back,
    total,
    elastic,
    mass,
    y_sems,
    x_sems,
    out_send_sems,
    out_recv_sems,
    back_send_sems,
    back_recv_sems,
):
    copies = {}
    for index, name in enumerate(operand_order):
        copies[name] = pltpu.make_async_copy(sources[index], local[name], in_sems.at[index])
        copies[name].start()
    displacement_ref, load_ref, density_ref = (
        local["displacement"],
        local["load"],
        local["density"],
    )
    class_ref, element_ref, coords_ref = local["class"], local["element"], local["coords"]
    slot_ref, angle_ref, stiffness_ref = local["slot"], local["angle"], local["stiffness"]
    _, width, height, depth = displacement_ref.shape
    rows = fields.shape[2]
    cap = recv_out.shape[2]
    slot_rows = cap // lanes
    all_rows = parts * slot_rows
    fibres = slot_ref.shape[0]
    me = lax.axis_index("dom")
    column = lax.axis_index("blk")

    barrier = pltpu.get_barrier_semaphore()

    def greet(step, carry):
        other = lax.rem(me + step, parts)
        pl.semaphore_signal(barrier, inc=1, device_id=(other, column), device_id_type=MESH)
        return carry

    lax.fori_loop(1, parts, greet, 0)

    @pl.when(column > 0)
    def _():
        pl.semaphore_signal(barrier, inc=1, device_id=(me, column - 1), device_id_type=MESH)

    @pl.when(column < columns - 1)
    def _():
        pl.semaphore_signal(barrier, inc=1, device_id=(me, column + 1), device_id_type=MESH)

    for name in ("element", "coords", "displacement"):
        copies[name].wait()

    def weigh(part, carry):
        span = pl.ds(pl.multiple_of(part * cap, lanes), cap)
        element = element_ref[:, span]
        along_x = quotient(element, height * depth)
        along_y = quotient(element - along_x * (height * depth), depth)
        along_z = element - along_x * (height * depth) - along_y * depth

        def weights(lowest, along, count):
            positions = lax.broadcasted_iota(jnp.int32, (count, cap), 0)
            upper = jnp.where(positions == lowest + 1, along, 0.0)
            return jnp.where(positions == lowest, 1.0 - along, upper)

        weight_x[:, span] = weights(along_x, coords_ref[0, :, span], width)
        weight_y[:, span] = weights(along_y, coords_ref[1, :, span], height)
        high, low = halves(weights(along_z, coords_ref[2, :, span], depth))
        weight_z[0:depth, span] = high
        weight_z[depth : 2 * depth, span] = low
        return carry

    lax.fori_loop(0, parts, weigh, 0)

    def barrier_count():
        return (
            parts
            - 1
            + jnp.where(column > 0, 1, 0)
            + jnp.where(column < columns - 1, 1, 0)
        )

    pl.semaphore_wait(barrier, barrier_count())

    def y_copy(side):
        return pltpu.make_async_remote_copy(
            src_ref=y_send.at[side],
            dst_ref=y_recv.at[1 - side],
            send_sem=y_sems.at[side],
            recv_sem=y_sems.at[3 - side],
            device_id=(me, column - 1 if side == 0 else column + 1),
            device_id_type=MESH,
        )

    def x_copy(side):
        return pltpu.make_async_remote_copy(
            src_ref=fields.at[1 if side == 0 else width],
            dst_ref=x_recv.at[1 - side],
            send_sem=x_sems.at[side],
            recv_sem=x_sems.at[3 - side],
            device_id=(me - 1 if side == 0 else me + 1, column),
            device_id_type=MESH,
        )

    y_there = (column > 0, column < columns - 1)
    x_there = (me > 0, me < parts - 1)
    def slot_copy(source, target, send_sems, recv_sems, other, slot):
        return pltpu.make_async_remote_copy(
            src_ref=source.at[other],
            dst_ref=target.at[slot],
            send_sem=send_sems.at[other],
            recv_sem=recv_sems.at[slot],
            device_id=(other, column),
            device_id_type=MESH,
        )

    high, low = halves(displacement_ref[...].reshape(3 * width * height, depth))
    count = 3 * width * height
    both = jnp.concatenate([high, low], axis=0)
    both = jnp.concatenate([both, both], axis=1)

    def planar_weights(span):
        planar = weight_x[:, span][:, None, :] * weight_y[:, span][None]
        return planar.reshape(width * height, cap)

    def interpolate(step, carry):
        other = lax.rem(me + step, parts)
        span = pl.ds(pl.multiple_of(other * cap, lanes), cap)
        sums = dot(both, weight_z[:, span])
        sums = sums[:count] + sums[count:]
        planar = planar_weights(span)
        for field in range(3):
            piece = sums[field * width * height : (field + 1) * width * height]
            send_out[other, field : field + 1, :] = jnp.sum(piece * planar, axis=0, keepdims=True)

        @pl.when(other != me)
        def _():
            slot_copy(send_out, recv_out, out_send_sems, out_recv_sems, other, me).start()

        return carry

    lax.fori_loop(1, parts + 1, interpolate, 0)
    recv_out[me] = send_out[me]

    for name in ("density", "class"):
        copies[name].wait()

    block_of = quotient(lax.broadcasted_iota(jnp.int32, (1, depth), 1), block_edge)
    for x_block in range(width // block_edge):
        for y_block in range(height // block_edge):
            kinds = class_ref[x_block, y_block : y_block + 1, :]
            classes = jnp.zeros((1, depth), jnp.int32)
            for z_block in range(depth // block_edge):
                classes = jnp.where(block_of == z_block, kinds[:, z_block : z_block + 1], classes)
            factor = jnp.zeros((1, depth), jnp.float32)
            for index, value in enumerate(class_values):
                factor = jnp.where(classes == index, jnp.float32(value), factor)
            span = slice(y_block * block_edge, (y_block + 1) * block_edge)
            for x in range(x_block * block_edge, (x_block + 1) * block_edge):
                density = density_ref[x, span, :]
                fields[x + 1, 3, span, :] = factor * density * density
                fields[x + 1, 4, span, :] = density
    blank = jnp.zeros((rows - height, depth), jnp.float32)
    for x in range(width):
        for field in range(3):
            fields[x + 1, field, 0:height, :] = displacement_ref[field, x]
        for field in range(5):
            fields[x + 1, field, height:rows, :] = blank
    for x in range(width):
        for field in range(5):
            y_send[0, field, x : x + 1, :] = fields[x + 1, field, 0:1, :]
            y_send[1, field, x : x + 1, :] = fields[x + 1, field, height - 1 : height, :]

    for side in range(2):

        @pl.when(y_there[side])
        def _():
            y_copy(side).start()

    for name in ("slot", "angle", "stiffness", "load"):
        copies[name].wait()
    diagonal = lax.broadcasted_iota(jnp.int32, (fibres, fibres), 0) == lax.broadcasted_iota(
        jnp.int32, (fibres, fibres), 1
    )
    stiffness = jnp.sum(jnp.where(diagonal, stiffness_ref[...], 0.0), axis=1, keepdims=True)
    slots = jnp.concatenate([slot_ref[fibre] for fibre in range(fibres)], axis=1)
    slot_row = quotient(slots, lanes)
    slot_lane = slots - slot_row * lanes
    lane_count = lax.broadcasted_iota(jnp.int32, (lanes, slots.shape[1]), 0)
    onehot[...] = jnp.where(lane_count == slot_lane, 1.0, 0.0).astype(jnp.bfloat16)
    in_row = lax.broadcasted_iota(jnp.int32, (all_rows, slots.shape[1]), 0) == slot_row
    for fibre in range(fibres):
        for index in range(2):
            angles[index, fibre : fibre + 1, :] = angle_ref[index, fibre]
    azimuth, elevation = angles[0], angles[1]
    flat = jnp.cos(elevation)
    direction = (jnp.cos(azimuth) * flat, jnp.sin(azimuth) * flat, jnp.sin(elevation))

    for side in range(2):

        @pl.when(y_there[side])
        def _():
            y_copy(1 - side).wait_recv()

        @pl.when(jnp.logical_not(y_there[side]))
        def _():
            y_recv[side] = jnp.zeros(y_recv.shape[1:], jnp.float32)

    for x in range(width):
        for field in range(5):
            fields[x + 1, field, rows - 1 : rows, :] = y_recv[0, field, x : x + 1, :]
            fields[x + 1, field, height : height + 1, :] = y_recv[1, field, x : x + 1, :]
    for side in range(2):

        @pl.when(x_there[side])
        def _():
            x_copy(side).start()

    def await_out(step, carry):
        other = lax.rem(me + step, parts)
        slot_copy(send_out, recv_out, out_send_sems, out_recv_sems, other, other).wait_recv()
        return carry

    lax.fori_loop(1, parts, await_out, 0)

    for field in range(3):
        for part in range(parts):
            for row in range(slot_rows):
                place = field * all_rows + part * slot_rows + row
                picked[place : place + 1, :] = recv_out[
                    part, field : field + 1, row * lanes : (row + 1) * lanes
                ]
    near, rest = halves(picked[...])
    chosen = dot(jnp.concatenate([near, rest], axis=0), onehot[...])
    chosen = chosen[: 3 * all_rows] + chosen[3 * all_rows :]
    segments = angles.shape[2]
    for field in range(3):
        piece = chosen[field * all_rows : (field + 1) * all_rows]
        line = jnp.sum(jnp.where(in_row, piece, 0.0), axis=0, keepdims=True)
        for fibre in range(fibres):
            nodes[field, fibre : fibre + 1, :] = line[:, fibre * segments : (fibre + 1) * segments]
    along = jnp.zeros((fibres, segments), jnp.float32)
    for field in range(3):
        place = nodes[field]
        along = along + direction[field] * (pltpu.roll(place, segments - 1, 1) - place)
    live = lax.broadcasted_iota(jnp.int32, along.shape, 1) < segments - 1
    tension = jnp.where(live, stiffness * jnp.maximum(along, 0.0), 0.0)
    terms = []
    for field in range(3):
        pull = tension * direction[field]
        nodes[field] = pull - pltpu.roll(pull, 1, 1)
        line = jnp.concatenate(
            [nodes[field, fibre : fibre + 1, :] for fibre in range(fibres)], axis=1
        )
        terms.append(jnp.where(in_row, line, 0.0))
    near, rest = halves(jnp.concatenate(terms, axis=0))
    sums = dot_t(jnp.concatenate([near, rest], axis=0), onehot[...])
    picked[...] = sums[: 3 * all_rows] + sums[3 * all_rows :]
    for field in range(3):
        for part in range(parts):
            for row in range(slot_rows):
                place = field * all_rows + part * slot_rows + row
                send_back[part, field : field + 1, row * lanes : (row + 1) * lanes] = picked[
                    place : place + 1, :
                ]

    def give_back(step, carry):
        other = lax.rem(me + step, parts)
        slot_copy(send_back, recv_back, back_send_sems, back_recv_sems, other, me).start()
        return carry

    lax.fori_loop(1, parts, give_back, 0)
    recv_back[me] = send_back[me]

    for side in range(2):
        edge = 0 if side == 0 else width + 1

        @pl.when(x_there[side])
        def _():
            x_copy(1 - side).wait_recv()
            fields[edge] = x_recv[side]

        @pl.when(jnp.logical_not(x_there[side]))
        def _():
            fields[edge] = jnp.zeros(fields.shape[1:], jnp.float32)

    table = mode_stiffness()
    level = lax.broadcasted_iota(jnp.int32, (rows, depth), 1)

    def plane_modes(plane):
        modes = []
        for field in range(3):
            value = fields[plane, field]
            above = jnp.where(level < depth - 1, pltpu.roll(value, depth - 1, 1), 0.0)
            pair = (value + above, above - value)
            beside = [pltpu.roll(item, rows - 1, 0) for item in pair]
            modes.append(
                [pair[0] + beside[0], pair[1] + beside[1], beside[0] - pair[0], beside[1] - pair[1]]
            )
        return modes

    def lift(value):
        return jnp.where(level > 0, pltpu.roll(value, 1, 1), 0.0)

    def layer(plane, carry):
        near_modes, far_modes = plane_modes(plane), plane_modes(plane + 1)
        modes = [None] * 24
        for field in range(3):
            for mode in range(4):
                low_side, high_side = near_modes[field][mode], far_modes[field][mode]
                modes[3 * mode + field] = high_side + low_side
                modes[3 * (mode + 4) + field] = high_side - low_side
        modulus = fields[plane, 3]
        forces = []
        for row in range(24):
            force = None
            for place in range(24):
                if table[row, place] != 0.0:
                    term = jnp.float32(table[row, place]) * modes[place]
                    force = term if force is None else force + term
            forces.append(None if force is None else force * modulus)
        passed = []
        for field in range(3):
            joined = []
            for mode in range(4):
                even, odd = forces[3 * mode + field], forces[3 * (mode + 4) + field]
                even = jnp.zeros_like(odd) if even is None else even
                joined.append(carry[4 * field + mode] + even - odd)
                passed.append(even + odd)
            flat_z = []
            for mode in range(2):
                even, odd = joined[mode], joined[mode + 2]
                flat_z.append(even - odd + pltpu.roll(even + odd, 1, 0))
            result = flat_z[0] - flat_z[1] + lift(flat_z[0] + flat_z[1])
            elastic[plane, field] = result[0:height]
        density = fields[plane, 4]
        density = density + pltpu.roll(density, 1, 0)
        density = density + lift(density)
        mass[plane] = 0.125 * (carry[12] + density)[0:height]
        return tuple(passed) + (density,)

    lax.fori_loop(
        0,
        width + 1,
        layer,
        tuple(jnp.zeros((rows, depth), jnp.float32) for _ in range(13)),
    )

    total[...] = jnp.zeros(total.shape, jnp.float32)

    def spread(step, carry):
        other = lax.rem(me + step, parts)

        @pl.when(other != me)
        def _():
            slot_copy(send_back, recv_back, back_send_sems, back_recv_sems, other, other).wait_recv()

        span = pl.ds(pl.multiple_of(other * cap, lanes), cap)
        force = recv_back[other]
        planar = planar_weights(span)
        near, rest = halves(
            jnp.concatenate([planar * force[field : field + 1] for field in range(3)], axis=0)
        )
        total[...] += dot_t(jnp.concatenate([near, rest], axis=0), weight_z[:, span])
        return carry

    lax.fori_loop(0, parts, spread, 0)
    fibre = (
        total[0:count, 0:depth]
        + total[0:count, depth : 2 * depth]
        + total[count : 2 * count, 0:depth]
        + total[count : 2 * count, depth : 2 * depth]
    ).reshape(3, width, height, depth)
    weight = mass[1 : width + 1]
    for field in range(3):
        ratio_ref[field] = (
            load_ref[field] - elastic[1 : width + 1, field] + fibre[field]
        ) / weight

    for side in range(2):

        @pl.when(y_there[side])
        def _():
            y_copy(side).wait_send()

        @pl.when(x_there[side])
        def _():
            x_copy(side).wait_send()

    def await_sends(step, carry):
        other = lax.rem(me + step, parts)
        slot_copy(send_out, recv_out, out_send_sems, out_recv_sems, other, me).wait_send()
        slot_copy(send_back, recv_back, back_send_sems, back_recv_sems, other, me).wait_send()
        return carry

    lax.fori_loop(1, parts, await_sends, 0)


def shards(
    displacement,
    velocity,
    load,
    density,
    block_class,
    host_element,
    host_coords,
    fibre_slot,
    fibre_angles,
    fibre_stiffness,
):
    _, width, height, depth = displacement.shape
    parts = lax.axis_size("dom")
    columns = lax.axis_size("blk")
    slots = host_element.shape[1]
    cap = slots // parts
    fibres, _, count = fibre_slot.shape
    rows = height + 8
    f32 = jnp.float32
    vmem = pl.BlockSpec(memory_space=pltpu.VMEM)
    boxes = pltpu.VMEM((parts, 3, cap), f32)
    operands = (
        displacement,
        density,
        block_class,
        host_element,
        host_coords,
        fibre_slot,
        fibre_angles,
        fibre_stiffness.reshape(1, fibres),
        load,
    )
    ratio = pl.pallas_call(
        functools.partial(kernel, parts, columns),
        out_shape=pltpu.VMEM(displacement.shape, f32),
        in_specs=[pl.BlockSpec(memory_space=pltpu.HBM)] * len(operands),
        out_specs=vmem,
        scratch_shapes=[pltpu.VMEM(operand.shape, operand.dtype) for operand in operands]
        + [
            pltpu.SemaphoreType.DMA((len(operands),)),
            pltpu.VMEM((width + 2, 5, rows, depth), f32),
            pltpu.VMEM((2, 5, width, depth), f32),
            pltpu.VMEM((2, 5, width, depth), f32),
            pltpu.VMEM((2, 5, rows, depth), f32),
            pltpu.VMEM((2 * depth, slots), jnp.bfloat16),
            pltpu.VMEM((width, slots), f32),
            pltpu.VMEM((height, slots), f32),
            pltpu.VMEM((lanes, fibres * count), jnp.bfloat16),
            pltpu.VMEM((2, fibres, count), f32),
            pltpu.VMEM((3 * slots // lanes, lanes), f32),
            pltpu.VMEM((3, fibres, count), f32),
            boxes,
            boxes,
            boxes,
            boxes,
            pltpu.VMEM((6 * width * height, 2 * depth), f32),
            pltpu.VMEM((width + 1, 3, height, depth), f32),
            pltpu.VMEM((width + 1, height, depth), f32),
            pltpu.SemaphoreType.DMA((4,)),
            pltpu.SemaphoreType.DMA((4,)),
            pltpu.SemaphoreType.DMA((parts,)),
            pltpu.SemaphoreType.DMA((parts,)),
            pltpu.SemaphoreType.DMA((parts,)),
            pltpu.SemaphoreType.DMA((parts,)),
        ],
        compiler_params=pltpu.CompilerParams(
            collective_id=0, has_side_effects=True, vmem_limit_bytes=60 * 1024 * 1024
        ),
    )(*operands)
    new_velocity = velocity + time_step * (ratio - damping * velocity)
    return displacement + time_step * new_velocity, new_velocity


def solution(mesh):
    return jax.shard_map(
        shards,
        mesh=mesh,
        in_specs=(
            P(None, "dom", "blk", None),
            P(None, "dom", "blk", None),
            P(None, "dom", "blk", None),
            P("dom", "blk", None),
            P("dom", "blk", None),
            P("blk", "dom"),
            P(None, "blk", "dom"),
            P("dom", "blk", None),
            P(None, "dom", "blk", None),
            P("dom", "blk"),
        ),
        out_specs=(P(None, "dom", "blk", None), P(None, "dom", "blk", None)),
        check_vma=False,
    )
```
